128 devices in a mesh: frame: 16 (over x, z_hi, core), head: 8 (over y, z_lo).
Axes of the slice: x: 4, y: 4, z: 4 (z_hi: 2, z_lo: 2; z = z_hi * 2 + z_lo), core: 2. Of those that a mesh axis runs over, the one named last changes fastest.
Arguments:
- queries: bfloat16 [4, 4096, 4096], P(None, 'frame', 'head'), may hold values from -6 to 6
- keys: bfloat16 [4, 4096, 4096], P(None, 'frame', 'head'), may hold values from -6 to 6
- values: bfloat16 [4, 4096, 4096], P(None, 'frame', 'head'), may hold values from -6 to 6
- step_sizes: bfloat16 [4, 4096, 16], P(None, 'frame', 'head'), may hold values from 9e-05 to 1.25, as said below
- starts: int32 [4], replicated, may hold values from 0 to 15, as said below
- resets: int32 [4, 16], replicated, may hold values 0 or 1
- init_in: bfloat16 [16, 256, 1024], P('head'), may hold values from -0.375 to 0.375
- init_out: bfloat16 [16, 512, 256], P('head'), may hold values from -0.25 to 0.25
- gain: float32 [4096], P('head'), may hold values from 0.25 to 1.75
- out_proj: bfloat16 [4096, 5120], P('head'), may hold values from -0.125 to 0.125
Outputs:
- mixed_out: bfloat16 [4, 4096, 5120], P(None, 'frame', 'head')
The draws below stay inside these ranges and needn't reach their ends.
Inputs may be any that keep to these rules, and one draw needn't show every extreme that they name: `starts`: 4 distinct blocks. `step_sizes`: positive.
All inputs are finite; a program needn't handle non-finite values.
Results may differ from the reference program's by a relative error of at most 0.035.
Values may be sent and summed in bfloat16 or wider, within the bound.
A program may use at most 128 MiB of HBM per device.

```python
import math
import jax
import jax.numpy as jnp
from jax import lax

HS = 256
HID = 512
HEADS = 16
DW = 5120
VIDEO_COUNT = 4
SEG_ROWS = 256
SEGS = 16
VIDEO_TOKENS = 4096
N_HEAD = 8


def draw_step_sizes(key, part):
    random_key_base, random_key_noise, random_key_spikes = jax.random.split(key, 3)
    learning_rate_base = jnp.exp(jax.random.uniform(random_key_base, (VIDEO_COUNT, 1, HEADS), jnp.float32, math.log(0.0002), math.log(0.02)))
    random_noise = jnp.exp(jax.random.uniform(random_key_noise, (VIDEO_COUNT, VIDEO_TOKENS, HEADS), jnp.float32, math.log(0.5), math.log(2.0)))
    sudden_spikes = jnp.where(jax.random.uniform(random_key_spikes, (VIDEO_COUNT, VIDEO_TOKENS, 1), jnp.float32) < 3.0 / VIDEO_TOKENS, 30.0, 1.0)
    return (learning_rate_base * random_noise * sudden_spikes).astype(jnp.bfloat16)


def draw_starts(key, part):
    order = jax.random.permutation(jax.random.fold_in(key, 17), SEGS)
    return order[:VIDEO_COUNT].astype(jnp.int32)


def place_ends(result, key, least, high):
    spot = [jax.random.randint(jax.random.fold_in(key, axis), (), 0, length) for axis, length in enumerate(result.shape)]
    widest = result.shape.index(max(result.shape))
    next_to = spot[:widest] + [(spot[widest] + 1) % result.shape[widest]] + spot[widest + 1:]
    return result.at[tuple(spot)].set(least).at[tuple(next_to)].set(high)


def raised(values, key, source, target, parts, factor):
    owner, partner = [(jnp.arange(values.shape[axis_at]) // (values.shape[axis_at] // parts)).reshape([-1 if axis == axis_at else 1 for axis in range(values.ndim)]) for axis_at in (source, target)]
    chosen = jax.random.permutation(key, parts)[partner]
    strong = (owner == chosen) | (owner == (partner + parts // 2) % parts)
    return jnp.where(strong, factor * values, values)


def block_scale(own_key, extent, pieces, smallest, top_value):
    def one(dim, blocks):
        draws = jax.random.uniform(jax.random.fold_in(jax.random.fold_in(own_key, 6), dim), (blocks,), jnp.float32, smallest / len(pieces), top_value / len(pieces))
        return jnp.repeat(jnp.exp(draws), extent[dim] // blocks).reshape((-1,) + (1,) * (len(extent) - dim - 1))

    level = one(*pieces[0])
    for cut in pieces[1:]:
        level = level * one(*cut)
    return level


def gaussian(key, extent, deviation, reach, pieces=(), kind=jnp.bfloat16):
    drawn = jax.random.normal(key, extent, jnp.float32) * deviation
    if len(pieces) > 0:
        drawn = block_scale(key, extent, pieces, -0.22, 0.18) * drawn
    return jnp.clip(drawn, min=-reach, max=reach).astype(kind)


def noise_with(key, extent, scale, limit, shards, heavy, kind=jnp.bfloat16):
    entries = scale * jax.random.normal(key, extent, jnp.float32)
    if shards:
        entries = entries * block_scale(key, extent, shards, -0.22, 0.18)
    return jnp.clip(raised(entries, jax.random.fold_in(key, 3), *heavy), -limit, limit).astype(kind)


def setup_inputs(seed: int = 0) -> dict:
    arg_keys = jax.random.split(jax.random.key(seed), 11)
    queries = gaussian(arg_keys[0], (VIDEO_COUNT, VIDEO_TOKENS, HEADS * HS), 1.0, 6.0, ((1, 16), (2, 8)))
    keys = gaussian(arg_keys[1], (VIDEO_COUNT, VIDEO_TOKENS, HEADS * HS), 1.0, 6.0, ((1, 16), (2, 8)))
    values = gaussian(arg_keys[2], (VIDEO_COUNT, VIDEO_TOKENS, HEADS * HS), 1.0, 6.0, ((1, 16), (2, 8)))
    step_sizes = draw_step_sizes(jax.random.fold_in(arg_keys[10], 71), 0)
    starts = draw_starts(jax.random.fold_in(arg_keys[10], 71), 0)
    resets = place_ends((jax.random.randint(arg_keys[5], (VIDEO_COUNT, SEGS), 0, 4) < 1).astype(jnp.int32), jax.random.fold_in(arg_keys[5], 1), 0, 1)
    init_in = gaussian(arg_keys[6], (HEADS, HS, 2 * HID), HS ** -0.5, 0.375, ((0, 8),))
    init_out = gaussian(arg_keys[7], (HEADS, HID, HS), HID ** -0.5, 0.25, ((0, 8),))
    gain = jnp.clip(1.0 + 0.15 * jax.random.normal(arg_keys[8], (HEADS * HS,), jnp.float32), 0.25, 1.75)
    out_proj = noise_with(arg_keys[9], (HEADS * HS, DW), (HEADS * HS) ** -0.5, 0.125, ((0, 8),), (0, 1, 8, 2.0))
    return dict(queries=queries, keys=keys, values=values, step_sizes=step_sizes, starts=starts, resets=resets, init_in=init_in, init_out=init_out, gain=gain, out_proj=out_proj)


def renorm(raw_weights, target):
    column_scale = target[:, None, :] * lax.rsqrt(lax.optimization_barrier(jnp.sum(raw_weights * raw_weights, axis=1, keepdims=True)) + 1e-06)
    return (raw_weights * column_scale).astype(jnp.bfloat16)

def advance(weights_in, weights_out, queries_seg, keys_seg, values_seg, rates_seg, norm_in, norm_out, gain):
    rows_here = queries_seg.shape[0]
    heads_here = weights_in.shape[0]
    head_width = weights_in.shape[1]
    hidden_width = weights_out.shape[1]
    key_heads = keys_seg.reshape(rows_here, heads_here, head_width).astype(jnp.float32)
    pre_keys = jnp.einsum('thd,hde->hte', key_heads, weights_in.astype(jnp.float32))
    first_half = pre_keys[..., :hidden_width]
    second_half = pre_keys[..., hidden_width:]
    sigmoid_first = jax.nn.sigmoid(first_half)
    activated = first_half * sigmoid_first
    hidden = (activated * second_half).astype(jnp.bfloat16)
    value_heads = values_seg.reshape(rows_here, heads_here, head_width).astype(jnp.float32)
    scaled = (value_heads * rates_seg.astype(jnp.float32)[:, :, None]).astype(jnp.bfloat16)
    grad_hidden = jnp.einsum('the,hfe->htf', scaled.astype(jnp.float32), weights_out.astype(jnp.float32))
    grad_first = grad_hidden * second_half * sigmoid_first * (1.0 + first_half * (1.0 - sigmoid_first))
    grad_second = grad_hidden * activated
    grad_pre = jnp.concatenate([grad_first, grad_second], axis=-1).astype(jnp.bfloat16)
    raw_in = weights_in.astype(jnp.float32) + jnp.einsum('thd,hte->hde', key_heads, grad_pre.astype(jnp.float32))
    raw_out = weights_out.astype(jnp.float32) + jnp.einsum('htf,the->hfe', hidden.astype(jnp.float32), scaled.astype(jnp.float32))
    new_in = renorm(raw_in, norm_in)
    new_out = renorm(raw_out, norm_out)
    query_heads = queries_seg.reshape(rows_here, heads_here, head_width).astype(jnp.float32)
    pre_queries = jnp.einsum('thd,hde->hte', query_heads, new_in.astype(jnp.float32))
    hidden_queries = (jax.nn.silu(pre_queries[..., :hidden_width]) * pre_queries[..., hidden_width:]).astype(jnp.bfloat16)
    fast_out = jnp.einsum('htf,hfe->the', hidden_queries.astype(jnp.float32), new_out.astype(jnp.float32))
    normed = fast_out * lax.rsqrt(lax.optimization_barrier(jnp.mean(fast_out * fast_out, axis=-1, keepdims=True)) + 1e-05)
    normed = normed * gain.reshape(heads_here, head_width)
    return (new_in, new_out, normed.reshape(rows_here, heads_here * head_width).astype(jnp.bfloat16))

def reference(queries, keys, values, step_sizes, starts, resets, init_in, init_out, gain, out_proj):
    norm_in = jnp.sqrt(lax.optimization_barrier(jnp.sum(jnp.square(init_in.astype(jnp.float32)), axis=1)))
    norm_out = jnp.sqrt(lax.optimization_barrier(jnp.sum(jnp.square(init_out.astype(jnp.float32)), axis=1)))

    def one_video(video_queries, video_keys, video_values, video_rates, first_block, reset_flags):

        def segment(loop_state, seg_index):
            state_in, state_out = loop_state
            block_now = (first_block + seg_index) % SEGS
            first_row = (block_now * SEG_ROWS).astype(jnp.int32)
            queries_seg = lax.dynamic_slice_in_dim(video_queries, first_row, SEG_ROWS, 0)
            keys_seg = lax.dynamic_slice_in_dim(video_keys, first_row, SEG_ROWS, 0)
            values_seg = lax.dynamic_slice_in_dim(video_values, first_row, SEG_ROWS, 0)
            rates_seg = lax.dynamic_slice_in_dim(video_rates, first_row, SEG_ROWS, 0)
            restart = jnp.logical_or(seg_index == 0, reset_flags[seg_index] == 1)
            weights_in = jnp.where(restart, init_in, state_in)
            weights_out = jnp.where(restart, init_out, state_out)
            new_in, new_out, normed = advance(weights_in, weights_out, queries_seg, keys_seg, values_seg, rates_seg, norm_in, norm_out, gain)
            return ((new_in, new_out), normed)
        _, outputs = lax.scan(segment, (init_in, init_out), jnp.arange(SEGS, dtype=jnp.int32))
        return jnp.roll(outputs, first_block, axis=0).reshape(VIDEO_TOKENS, HEADS * HS)
    normed_all = jax.vmap(one_video)(queries, keys, values, step_sizes, starts, resets)
    flat_rows = normed_all.reshape(VIDEO_COUNT * VIDEO_TOKENS, HEADS * HS)
    group_width = HEADS * HS // N_HEAD

    def add_group(running, group_index):
        slice_rows = lax.dynamic_slice_in_dim(flat_rows, (group_index * group_width).astype(jnp.int32), group_width, 1)
        slice_weights = lax.dynamic_slice_in_dim(out_proj, (group_index * group_width).astype(jnp.int32), group_width, 0)
        partial_value = jnp.dot(slice_rows, slice_weights, preferred_element_type=jnp.float32).astype(jnp.bfloat16)
        partial_value = lax.optimization_barrier(partial_value)
        return (running + partial_value.astype(jnp.float32), None)
    running, _ = lax.scan(add_group, jnp.zeros((VIDEO_COUNT * VIDEO_TOKENS, DW), jnp.float32), jnp.arange(N_HEAD, dtype=jnp.int32))
    return running.astype(jnp.bfloat16).reshape(VIDEO_COUNT, VIDEO_TOKENS, DW)
```

```python
import jax
import jax.numpy as jnp
from jax import lax
from jax.experimental import pallas as pl
from jax.experimental.pallas import tpu as pltpu
from jax.sharding import PartitionSpec as P

MESH = pl.DeviceIdType.MESH
BF16 = jnp.bfloat16
F32 = jnp.float32

VIDEOS = 4
ROWS = 256
SEGS = 16
HS = 256
HID = 512
CHIPS = 8
SLAB = 1280
OUT = 640


def tile(start, size):
    return pl.ds(pl.multiple_of(start, size), size)


def dot(a, b):
    return jnp.dot(a, b, preferred_element_type=F32)


def dot_t(a, b):
    return lax.dot_general(a, b, (((1,), (1,)), ((), ())), preferred_element_type=F32)


def sigmoid(x):
    return 0.5 * jnp.tanh(0.5 * x) + 0.5


def body(
    starts, resets, gain, steps, queries, keys, values, init_in, init_out, proj,
    out,
    v_buf, init_in_buf, init_out_buf, scaled, ks, kst, q_buf, state_in, state_out,
    normed, a_buf, slab, part_send, part_recv, own,
    local_sem, ks_send, ks_recv, fwd_send, fwd_recv, q_send, q_recv,
    a_send, a_recv, y_send, y_recv, w_send, w_recv, wf_send, wf_recv, z_send, z_recv,
):
    frame = lax.axis_index("frame")
    head = lax.axis_index("head")
    chip, core = frame // 2, frame % 2
    y, zl = head // 2, head % 2
    sibling = (chip * 2 + 1 - core, head)
    video, hh = chip // 2, chip % 2

    def peer(c):
        return (c * 2 + core, head)

    def y_peer(dy):
        return (frame, ((y + dy) % 4) * 2 + zl)

    z_peer = (frame, y * 2 + 1 - zl)

    def remote(src, dst, send, recv, where):
        return pltpu.make_async_remote_copy(
            src_ref=src, dst_ref=dst, send_sem=send, recv_sem=recv,
            device_id=where, device_id_type=MESH,
        )

    v_copy = pltpu.make_async_copy(values, v_buf, local_sem.at[0])
    ii_copy = pltpu.make_async_copy(init_in.at[hh], init_in_buf, local_sem.at[1])
    io_copy = pltpu.make_async_copy(init_out.at[hh], init_out_buf, local_sem.at[2])
    k_copy = pltpu.make_async_copy(
        keys.at[video, :, tile(hh * HS, HS)], ks.at[frame, 0], local_sem.at[3]
    )
    q_copy = pltpu.make_async_copy(
        queries.at[video, :, tile(hh * HS, HS)], q_buf.at[chip], local_sem.at[4]
    )
    w_copy = pltpu.make_async_copy(
        proj.at[:, tile(y * SLAB, SLAB)], slab.at[tile(y * 2 * HS, 2 * HS)], local_sem.at[5]
    )
    own_copy = pltpu.make_async_copy(
        normed.at[chip], a_buf.at[video, :, tile((y * 2 + hh) * HS, HS)], local_sem.at[6]
    )
    v_copy.start()
    k_copy.start()
    ii_copy.start()
    io_copy.start()
    q_copy.start()

    barrier = pltpu.get_barrier_semaphore()

    def greet(d, _):
        pl.semaphore_signal(barrier, inc=1, device_id=peer((chip + d) % CHIPS), device_id_type=MESH)
        return 0

    lax.fori_loop(1, CHIPS, greet, 0)
    pl.semaphore_signal(barrier, inc=1, device_id=sibling, device_id_type=MESH)
    pl.semaphore_signal(barrier, inc=1, device_id=z_peer, device_id_type=MESH)
    for dy in (1, 2, 3):
        pl.semaphore_signal(barrier, inc=1, device_id=y_peer(dy), device_id_type=MESH)
    pl.semaphore_wait(barrier, CHIPS - 1 + 5)

    def key_to(d):
        c = (chip + d) % CHIPS
        return remote(
            keys.at[c // 2, :, tile((c % 2) * HS, HS)], ks.at[frame, 0],
            ks_send.at[d, 0], ks_recv.at[chip, 0], peer(c),
        )

    def scaled_to(d):
        c = (chip + d) % CHIPS
        return remote(
            scaled.at[c], ks.at[frame, 1], ks_send.at[d, 1], ks_recv.at[chip, 1], peer(c)
        )

    def query_to(d):
        c = (chip + d) % CHIPS
        return remote(
            queries.at[c // 2, :, tile((c % 2) * HS, HS)], q_buf.at[chip],
            q_send.at[d], q_recv.at[chip], peer(c),
        )

    def start_all(make, low, high):
        def step(d, _):
            make(d).start()
            return 0

        lax.fori_loop(low, high, step, 0)

    def wait_send_all(make, low, high):
        def step(d, _):
            make(d).wait_send()
            return 0

        lax.fori_loop(low, high, step, 0)

    start_all(key_to, 1, CHIPS)

    def slab_rows(group, c):
        return slab.at[tile((group * 2 + c) * HS, HS)]

    def slab_to(dy):
        target = (y + dy) % 4
        return remote(
            proj.at[tile(core * HS, HS), tile(target * SLAB, SLAB)], slab_rows(y, core),
            w_send.at[dy], w_recv.at[y], y_peer(dy),
        )

    def slab_from(dy):
        group = (y + dy) % 4
        return remote(
            slab_rows(group, core), slab_rows(group, core),
            w_send.at[dy], w_recv.at[group], y_peer(dy),
        )

    def slab_on(dy):
        group = (y + dy) % 4
        return remote(
            slab_rows(group, core), slab_rows(group, core),
            wf_send.at[dy], wf_recv.at[group], sibling,
        )

    def slab_off(dy):
        group = (y + dy) % 4
        return remote(
            slab_rows(group, 1 - core), slab_rows(group, 1 - core),
            wf_send.at[dy], wf_recv.at[group], sibling,
        )

    v_copy.wait()
    for b in range(VIDEOS):
        for h in range(2):
            rate = steps[b, :, h : h + 1].astype(F32)
            scaled[b * 2 + h] = (v_buf[b, :, h * HS : (h + 1) * HS].astype(F32) * rate).astype(BF16)
    start_all(scaled_to, 1, CHIPS)
    w_copy.start()
    start_all(slab_to, 1, 4)

    ks[frame, 1] = scaled[chip]
    k_copy.wait()

    def hand_on(c):
        slot = c * 2 + core
        return remote(ks.at[slot], ks.at[slot], fwd_send.at[c], fwd_recv.at[c], sibling)

    def handed(c):
        slot = c * 2 + 1 - core
        return remote(ks.at[slot], ks.at[slot], fwd_send.at[c], fwd_recv.at[c], sibling)

    hand_on(chip).start()
    ii_copy.wait()
    io_copy.wait()
    state_in[SEGS] = init_in_buf[...]
    state_out[SEGS] = init_out_buf[...].T
    wide = init_in_buf[...].astype(F32)
    norm_in = jnp.sqrt(jnp.sum(wide * wide, axis=0, keepdims=True))
    wide = state_out[SEGS].astype(F32)
    norm_out = jnp.sqrt(jnp.sum(wide * wide, axis=1, keepdims=True))

    def turn(slot):
        kst[slot, 0] = ks[slot, 0].T
        kst[slot, 1] = ks[slot, 1].T

    turn(frame)

    def key_from(c, which):
        slot = c * 2 + core
        return remote(
            ks.at[slot, which], ks.at[slot, which], ks_send.at[0, which], ks_recv.at[c, which], peer(c)
        )

    def take(d, _):
        c = (chip + CHIPS - d) % CHIPS
        key_from(c, 0).wait_recv()
        key_from(c, 1).wait_recv()
        hand_on(c).start()
        turn(c * 2 + core)
        back = (c + 1) % CHIPS
        handed(back).wait_recv()
        turn(back * 2 + 1 - core)
        return 0

    lax.fori_loop(1, CHIPS, take, 0)
    start_all(query_to, 1, CHIPS)
    last = (chip + 1) % CHIPS
    handed(last).wait_recv()
    turn(last * 2 + 1 - core)

    start = starts[video]

    def segment(s, _):
        block = lax.rem(start + s, SEGS)
        restart = jnp.logical_or(s == 0, resets[video, s] == 1)
        before = jnp.where(restart, SEGS, s - 1)
        key, scl = ks[block, 0], ks[block, 1]
        w_in = state_in[before]
        w_out = state_out[before]
        pre = dot(key, w_in)
        grad = dot(scl, w_out)
        h1, h3 = pre[:, :HID], pre[:, HID:]
        sig = sigmoid(h1)
        act = h1 * sig
        hidden = (act * h3).astype(BF16)
        d1 = (grad * h3 * (sig + act * (1.0 - sig))).astype(BF16)
        d3 = (grad * act).astype(BF16)
        raw_out = w_out.astype(F32) + dot(kst[block, 1], hidden)
        scale = norm_out * lax.rsqrt(jnp.sum(raw_out * raw_out, axis=1, keepdims=True) + 1e-06)
        state_out[s] = (raw_out * scale).astype(BF16)
        turned = kst[block, 0]
        for half, d in ((0, d1), (1, d3)):
            at = slice(half * HID, (half + 1) * HID)
            raw = w_in[:, at].astype(F32) + dot(turned, d)
            scale = norm_in[:, at] * lax.rsqrt(jnp.sum(raw * raw, axis=0, keepdims=True) + 1e-06)
            state_in[s, :, at] = (raw * scale).astype(BF16)
        return 0

    lax.fori_loop(0, SEGS, segment, 0)

    def query_from(c):
        return remote(q_buf.at[c], q_buf.at[c], q_send.at[0], q_recv.at[c], peer(c))

    def columns_of(group, c):
        return a_buf.at[c // 2, :, tile((group * 2 + c % 2) * HS, HS)]

    def normed_to(d):
        c = (chip + d) % CHIPS
        return remote(
            normed.at[c], columns_of(y, chip), a_send.at[d], a_recv.at[chip], peer(c)
        )

    def normed_from(c):
        return remote(
            columns_of(y, c), columns_of(y, c), a_send.at[0], a_recv.at[c], peer(c)
        )

    def spread(c, dy):
        return remote(
            columns_of(y, c), columns_of(y, c), y_send.at[dy, c], y_recv.at[y, c], y_peer(dy)
        )

    def gathered(c, group):
        return remote(
            columns_of(group, c), columns_of(group, c),
            y_send.at[0, c], y_recv.at[group, c], y_peer(1),
        )

    gain_row = gain[pl.ds(hh, 1), :]
    q_copy.wait()

    def query(d, _):
        c = (chip + d) % CHIPS

        @pl.when(d > 0)
        def _():
            query_from(c).wait_recv()

        done = lax.rem(c * 2 + core + SEGS - start, SEGS)
        pre = dot(q_buf[c], state_in[done])
        h1, h3 = pre[:, :HID], pre[:, HID:]
        hidden = (h1 * sigmoid(h1) * h3).astype(BF16)
        fast = dot_t(hidden, state_out[done])
        fast = fast * lax.rsqrt(jnp.mean(fast * fast, axis=1, keepdims=True) + 1e-05)
        normed[c] = (fast * gain_row).astype(BF16)

        @pl.when(d > 0)
        def _():
            normed_to(d).start()

        @pl.when(d == 0)
        def _():
            own_copy.start()
            own_copy.wait()
            for dy in (1, 3, 2):
                spread(c, dy).start()

        return 0

    lax.fori_loop(0, CHIPS, query, 0)

    for dy in (1, 3, 2):
        slab_from(dy).wait_recv()
        slab_on(dy).start()
    w_copy.wait()

    def pass_on(d, _):
        c = (chip + CHIPS - d) % CHIPS
        normed_from(c).wait_recv()
        for dy in (1, 3, 2):
            spread(c, dy).start()
        return 0

    lax.fori_loop(1, CHIPS, pass_on, 0)
    for dy in (1, 2, 3):
        slab_off(dy).wait_recv()

    def part_to(b):
        return remote(part_send.at[b], part_recv.at[b], z_send.at[b], z_recv.at[b], z_peer)

    def nth(n):
        return (chip // 2 + 3 - n + chip % 2) % VIDEOS

    def project(n, _):
        b = nth(n)
        for h in range(2):
            for dy in (1, 2, 3):
                gathered(b * 2 + h, (y + dy) % 4).wait_recv()
        rows = a_buf[b]
        part_send[b] = dot(rows, slab[:, tile((1 - zl) * OUT, OUT)]).astype(BF16)
        part_to(b).start()
        own[b] = dot(rows, slab[:, tile(zl * OUT, OUT)])
        return 0

    lax.fori_loop(0, VIDEOS, project, 0)

    def finish(n, _):
        b = nth(n)
        part_to(b).wait_recv()
        out[b] = (own[b] + part_recv[b].astype(F32)).astype(BF16)
        return 0

    lax.fori_loop(0, VIDEOS, finish, 0)

    wait_send_all(key_to, 1, CHIPS)
    wait_send_all(scaled_to, 1, CHIPS)
    wait_send_all(query_to, 1, CHIPS)
    wait_send_all(normed_to, 1, CHIPS)
    wait_send_all(slab_to, 1, 4)
    wait_send_all(slab_on, 1, 4)
    wait_send_all(hand_on, 0, CHIPS)
    wait_send_all(part_to, 0, VIDEOS)

    def sent(c, _):
        for dy in (1, 2, 3):
            spread(c, dy).wait_send()
        return 0

    lax.fori_loop(0, CHIPS, sent, 0)


def shards(queries, keys, values, step_sizes, starts, resets, init_in, init_out, gain, out_proj):
    anywhere = pl.BlockSpec(memory_space=pl.ANY)
    vmem = pl.BlockSpec(memory_space=pltpu.VMEM)
    smem = pl.BlockSpec(memory_space=pltpu.SMEM)
    dma = pltpu.SemaphoreType.DMA
    return pl.pallas_call(
        body,
        name="layer",
        out_shape=jax.ShapeDtypeStruct((VIDEOS, ROWS, OUT), BF16),
        in_specs=[smem, smem, vmem, vmem] + [anywhere] * 6,
        out_specs=vmem,
        scratch_shapes=[
            pltpu.VMEM((VIDEOS, ROWS, 2 * HS), BF16),
            pltpu.VMEM((HS, 2 * HID), BF16),
            pltpu.VMEM((HID, HS), BF16),
            pltpu.VMEM((CHIPS, ROWS, HS), BF16),
            pltpu.VMEM((SEGS, 2, ROWS, HS), BF16),
            pltpu.VMEM((SEGS, 2, HS, ROWS), BF16),
            pltpu.VMEM((CHIPS, ROWS, HS), BF16),
            pltpu.VMEM((SEGS + 1, HS, 2 * HID), BF16),
            pltpu.VMEM((SEGS + 1, HS, HID), BF16),
            pltpu.VMEM((CHIPS, ROWS, HS), BF16),
            pltpu.VMEM((VIDEOS, ROWS, 4 * 2 * HS), BF16),
            pltpu.VMEM((4 * 2 * HS, SLAB), BF16),
            pltpu.VMEM((VIDEOS, ROWS, OUT), BF16),
            pltpu.VMEM((VIDEOS, ROWS, OUT), BF16),
            pltpu.VMEM((VIDEOS, ROWS, OUT), F32),
            dma((7,)),
            dma((CHIPS, 2)), dma((CHIPS, 2)),
            dma((CHIPS,)), dma((CHIPS,)),
            dma((CHIPS,)), dma((CHIPS,)),
            dma((CHIPS,)), dma((CHIPS,)),
            dma((4, CHIPS)), dma((4, CHIPS)),
            dma((4,)), dma((4,)),
            dma((4,)), dma((4,)),
            dma((VIDEOS,)), dma((VIDEOS,)),
        ],
        compiler_params=pltpu.CompilerParams(
            collective_id=0, has_side_effects=True, vmem_limit_bytes=60 * 1024 * 1024
        ),
    )(
        starts, resets, gain.reshape(2, HS), step_sizes,
        queries, keys, values, init_in, init_out, out_proj,
    )


def solution(mesh):
    rows = P(None, "frame", "head")
    return jax.shard_map(
        shards,
        mesh=mesh,
        in_specs=(
            rows, rows, rows, rows, P(), P(),
            P("head", None, None), P("head", None, None), P("head"), P("head", None),
        ),
        out_specs=rows,
        check_vma=False,
    )
```

```python
import jax
import jax.numpy as jnp
from jax import lax
from jax.experimental import pallas as pl
from jax.experimental.pallas import tpu as pltpu
from jax.sharding import PartitionSpec as P

MESH = pl.DeviceIdType.MESH
BF16 = jnp.bfloat16
F32 = jnp.float32

VIDEOS = 4
ROWS = 256
SEGS = 16
HS = 256
HID = 512
CHIPS = 8
FRONT = ((1, 1), (3, 0), (3, 1), (1, 0), (2, 0), (0, 1), (2, 1))
WINDOW = 4
SLAB = 1280
OUT = 640


def tile(start, size):
    return pl.ds(pl.multiple_of(start, size), size)


def dot(a, b):
    return jnp.dot(a, b, preferred_element_type=F32)


def dot_t(a, b):
    return lax.dot_general(a, b, (((1,), (1,)), ((), ())), preferred_element_type=F32)


def sigmoid(x):
    return 0.5 * jnp.tanh(0.5 * x) + 0.5


def body(
    starts, resets, gain, steps, queries, keys, values, init_in, init_out, proj,
    own_out, part_out,
    v_buf, init_in_buf, init_out_buf, scaled, ks, kst, q_buf, state_in, state_out,
    normed, a_buf, slab, part_send, own,
    local_sem, ks_send, ks_recv, fwd_send, fwd_recv, q_send, q_recv,
    a_send, a_recv, y_send, y_recv, w_send, w_recv, wf_send, wf_recv, z_send, z_recv, own_sem,
):
    frame = lax.axis_index("frame")
    head = lax.axis_index("head")
    chip, core = frame // 2, frame % 2
    y, zl = head // 2, head % 2
    sibling = (chip * 2 + 1 - core, head)
    video, hh = chip // 2, chip % 2

    def peer(c):
        return (c * 2 + core, head)

    def ahead(dx, dz):
        return (video + dx) % 4 * 2 + (hh + dz) % 2

    def behind(dx, dz):
        return (video + 4 - dx) % 4 * 2 + (hh + 2 - dz) % 2

    def y_peer(dy):
        return (frame, ((y + dy) % 4) * 2 + zl)

    z_peer = (frame, y * 2 + 1 - zl)

    def remote(src, dst, send, recv, where):
        return pltpu.make_async_remote_copy(
            src_ref=src, dst_ref=dst, send_sem=send, recv_sem=recv,
            device_id=where, device_id_type=MESH,
        )

    v_copy = pltpu.make_async_copy(values, v_buf, local_sem.at[0])
    ii_copy = pltpu.make_async_copy(init_in.at[hh], init_in_buf, local_sem.at[1])
    io_copy = pltpu.make_async_copy(init_out.at[hh], init_out_buf, local_sem.at[2])
    k_copy = pltpu.make_async_copy(
        keys.at[video, :, tile(hh * HS, HS)], ks.at[frame, 0], local_sem.at[3]
    )
    q_copy = pltpu.make_async_copy(
        queries.at[video, :, tile(hh * HS, HS)], q_buf.at[chip], local_sem.at[4]
    )
    w_copy = pltpu.make_async_copy(
        proj.at[:, tile(y * SLAB, SLAB)], slab.at[tile(y * 2 * HS, 2 * HS)], local_sem.at[5]
    )
    own_copy = pltpu.make_async_copy(
        normed.at[chip], a_buf.at[video, :, tile((y * 2 + hh) * HS, HS)], local_sem.at[6]
    )
    v_copy.start()
    k_copy.start()
    ii_copy.start()
    io_copy.start()
    q_copy.start()

    barrier = pltpu.get_barrier_semaphore()

    def greet(d, _):
        pl.semaphore_signal(barrier, inc=1, device_id=peer((chip + d) % CHIPS), device_id_type=MESH)
        return 0

    lax.fori_loop(1, CHIPS, greet, 0)
    pl.semaphore_signal(barrier, inc=1, device_id=sibling, device_id_type=MESH)
    pl.semaphore_signal(barrier, inc=1, device_id=z_peer, device_id_type=MESH)
    for dy in (1, 2, 3):
        pl.semaphore_signal(barrier, inc=1, device_id=y_peer(dy), device_id_type=MESH)
    pl.semaphore_wait(barrier, CHIPS - 1 + 5)

    def key_to(c):
        return remote(
            keys.at[c // 2, :, tile((c % 2) * HS, HS)], ks.at[frame, 0],
            ks_send.at[c, 0], ks_recv.at[chip, 0], peer(c),
        )

    def scaled_to(c):
        return remote(
            scaled.at[c], ks.at[frame, 1], ks_send.at[c, 1], ks_recv.at[chip, 1], peer(c)
        )

    def query_to(c):
        return remote(
            queries.at[c // 2, :, tile((c % 2) * HS, HS)], q_buf.at[chip],
            q_send.at[c], q_recv.at[chip], peer(c),
        )

    for shift in FRONT[:WINDOW]:
        key_to(ahead(*shift)).start()

    def slab_rows(group, c):
        return slab.at[tile((group * 2 + c) * HS, HS)]

    def slab_to(dy):
        target = (y + dy) % 4
        return remote(
            proj.at[tile(core * HS, HS), tile(target * SLAB, SLAB)], slab_rows(y, core),
            w_send.at[dy], w_recv.at[y], y_peer(dy),
        )

    def slab_from(dy):
        group = (y + dy) % 4
        return remote(
            slab_rows(group, core), slab_rows(group, core),
            w_send.at[dy], w_recv.at[group], y_peer(dy),
        )

    def slab_on(dy):
        group = (y + dy) % 4
        return remote(
            slab_rows(group, core), slab_rows(group, core),
            wf_send.at[dy], wf_recv.at[group], sibling,
        )

    def slab_off(dy):
        group = (y + dy) % 4
        return remote(
            slab_rows(group, 1 - core), slab_rows(group, 1 - core),
            wf_send.at[dy], wf_recv.at[group], sibling,
        )

    v_copy.wait()
    rates = jnp.concatenate([steps[b].astype(F32) for b in range(VIDEOS)], axis=0).T
    for c in range(CHIPS):
        block = v_buf[c // 2, :, (c % 2) * HS : (c % 2 + 1) * HS].astype(F32)
        scaled[c] = (block * rates[:, c : c + 1]).astype(BF16)
    for shift in FRONT[:WINDOW]:
        scaled_to(ahead(*shift)).start()
    w_copy.start()
    for dy in (1, 3, 2):
        slab_to(dy).start()

    ks[frame, 1] = scaled[chip]
    k_copy.wait()

    def hand_on(c):
        slot = c * 2 + core
        return remote(ks.at[slot], ks.at[slot], fwd_send.at[c], fwd_recv.at[c], sibling)

    def handed(c):
        slot = c * 2 + 1 - core
        return remote(ks.at[slot], ks.at[slot], fwd_send.at[c], fwd_recv.at[c], sibling)

    hand_on(chip).start()
    ii_copy.wait()
    io_copy.wait()
    state_in[SEGS] = init_in_buf[...]
    state_out[SEGS] = init_out_buf[...].T
    wide = init_in_buf[...].astype(F32)
    norm_in = jnp.sqrt(jnp.sum(wide * wide, axis=0, keepdims=True))
    wide = state_out[SEGS].astype(F32)
    norm_out = jnp.sqrt(jnp.sum(wide * wide, axis=1, keepdims=True))

    def turn(slot):
        kst[slot, 0] = ks[slot, 0].T
        kst[slot, 1] = ks[slot, 1].T

    turn(frame)

    def key_from(c, which):
        slot = c * 2 + core
        return remote(
            ks.at[slot, which], ks.at[slot, which], ks_send.at[0, which], ks_recv.at[c, which], peer(c)
        )

    def take_handed(c):
        handed(c).wait_recv()
        turn(c * 2 + 1 - core)

    back = chip
    for n, shift in enumerate(FRONT):
        c = behind(*shift)
        key_from(c, 0).wait_recv()
        key_from(c, 1).wait_recv()
        hand_on(c).start()
        if n + WINDOW < len(FRONT):
            done, later = ahead(*shift), ahead(*FRONT[n + WINDOW])
            key_to(done).wait_send()
            scaled_to(done).wait_send()
            key_to(later).start()
            scaled_to(later).start()
        turn(c * 2 + core)
        take_handed(back)
        back = c
    for shift in FRONT:
        query_to(ahead(*shift)).start()
    take_handed(back)

    start = starts[video]

    def segment(s, _):
        block = lax.rem(start + s, SEGS)
        restart = jnp.logical_or(s == 0, resets[video, s] == 1)
        before = jnp.where(restart, SEGS, s - 1)
        key, scl = ks[block, 0], ks[block, 1]
        w_in = state_in[before]
        w_out = state_out[before]
        pre = dot(key, w_in)
        grad = dot(scl, w_out)
        h1, h3 = pre[:, :HID], pre[:, HID:]
        sig = sigmoid(h1)
        act = h1 * sig
        hidden = (act * h3).astype(BF16)
        d1 = (grad * h3 * (sig + act * (1.0 - sig))).astype(BF16)
        d3 = (grad * act).astype(BF16)
        raw_out = w_out.astype(F32) + dot(kst[block, 1], hidden)
        scale = norm_out * lax.rsqrt(jnp.sum(raw_out * raw_out, axis=1, keepdims=True) + 1e-06)
        state_out[s] = (raw_out * scale).astype(BF16)
        turned = kst[block, 0]
        for half, d in ((0, d1), (1, d3)):
            at = slice(half * HID, (half + 1) * HID)
            raw = w_in[:, at].astype(F32) + dot(turned, d)
            scale = norm_in[:, at] * lax.rsqrt(jnp.sum(raw * raw, axis=0, keepdims=True) + 1e-06)
            state_in[s, :, at] = (raw * scale).astype(BF16)
        return 0

    lax.fori_loop(0, SEGS, segment, 0)

    for dy in (1, 3, 2):
        slab_from(dy).wait_recv()
        slab_on(dy).start()

    def query_from(c):
        return remote(q_buf.at[c], q_buf.at[c], q_send.at[c], q_recv.at[c], peer(c))

    def columns_of(group, c):
        return a_buf.at[c // 2, :, tile((group * 2 + c % 2) * HS, HS)]

    def normed_to(c):
        return remote(
            normed.at[c], columns_of(y, chip), a_send.at[c], a_recv.at[chip], peer(c)
        )

    def normed_from(c):
        return remote(
            columns_of(y, c), columns_of(y, c), a_send.at[c], a_recv.at[c], peer(c)
        )

    def spread(c, dy):
        return remote(
            columns_of(y, c), columns_of(y, c), y_send.at[dy, c], y_recv.at[y, c], y_peer(dy)
        )

    def gathered(c, group):
        return remote(
            columns_of(group, c), columns_of(group, c),
            y_send.at[0, c], y_recv.at[group, c], y_peer(1),
        )

    gain_row = jnp.where(hh == 0, gain[:, :HS], gain[:, HS:])

    def query(c):
        done = lax.rem(c * 2 + core + SEGS - start, SEGS)
        pre = dot(q_buf[c], state_in[done])
        h1, h3 = pre[:, :HID], pre[:, HID:]
        hidden = (h1 * sigmoid(h1) * h3).astype(BF16)
        fast = dot_t(hidden, state_out[done])
        fast = fast * lax.rsqrt(jnp.mean(fast * fast, axis=1, keepdims=True) + 1e-05)
        normed[c] = (fast * gain_row).astype(BF16)

    def answer(c):
        query_from(c).wait_recv()
        query(c)
        normed_to(c).start()

    def answer_sides(n, _):
        answer(ahead(1 + n % 2 * 2, n // 2))
        return 0

    def answer_far(n, _):
        answer(ahead(2, n))
        return 0

    def nth(pair):
        return pair + pair // 2 - pair // 3 * 2

    def spread_all(c):
        for dy in (1, 3):
            spread(c, dy).start()

    def relay(c):
        group = (y + 3 + c % 2 * 2) % 4
        return remote(
            columns_of(group, c), columns_of(group, c),
            y_send.at[2, c], y_recv.at[group, c], (frame, ((y + 1 + c % 2 * 2) % 4) * 2 + zl),
        )

    def relay_on(n):
        c = behind(nth(n // 2), n % 2)
        gathered(c, (y + 3 + c % 2 * 2) % 4).wait_recv()
        relay(c).start()

    def pass_on(n):
        c = behind(nth(n // 2), n % 2)
        normed_from(c).wait_recv()

        @pl.when(n > 1)
        def _():
            earlier = behind(nth((n - 2) // 2), n % 2)
            for dy in (1, 3):
                spread(earlier, dy).wait_send()

        spread_all(c)

    def part_to(b):
        return remote(part_send.at[b], part_out.at[b], z_send.at[b], z_recv.at[b], z_peer)

    def own_to(b):
        return pltpu.make_async_copy(own.at[b], own_out.at[b], own_sem.at[b])

    def project(n):
        b = (video + 4 - nth(n)) % 4
        for h in range(2):
            for dy in (2, 1 + 2 * h):
                gathered(b * 2 + h, (y + dy) % 4).wait_recv()
        rows = a_buf[b]
        part_send[b] = dot(rows, slab[:, tile((1 - zl) * OUT, OUT)]).astype(BF16)
        part_to(b).start()
        own[b] = dot(rows, slab[:, tile(zl * OUT, OUT)]).astype(BF16)
        own_to(b).start()

    q_copy.wait()
    query(chip)
    own_copy.start()
    own_copy.wait()
    spread_all(chip)
    answer(ahead(0, 1))
    lax.fori_loop(0, 4, answer_sides, 0)
    lax.fori_loop(0, 2, answer_far, 0)
    w_copy.wait()
    for dy in (1, 2, 3):
        slab_off(dy).wait_recv()

    def turns(n, _):
        @pl.when(n < CHIPS)
        def _():
            pass_on(n)

        @pl.when(n <= CHIPS)
        def _():
            relay_on(n - 1)

        @pl.when(jnp.logical_and(n >= 3, n % 2 == 1))
        def _():
            project((n - 3) // 2)

        return 0

    lax.fori_loop(1, CHIPS + 2, turns, 0)

    def finish(b, _):
        part_to(b).wait_recv()
        own_to(b).wait()
        part_to(b).wait_send()
        return 0

    lax.fori_loop(0, VIDEOS, finish, 0)

    for shift in FRONT[len(FRONT) - WINDOW :]:
        key_to(ahead(*shift)).wait_send()
        scaled_to(ahead(*shift)).wait_send()

    def sent(d, _):
        c = (chip + d) % CHIPS
        query_to(c).wait_send()
        normed_to(c).wait_send()
        relay(c).wait_send()
        return 0

    lax.fori_loop(1, CHIPS, sent, 0)
    relay(chip).wait_send()
    for dy in (1, 2, 3):
        slab_to(dy).wait_send()
        slab_on(dy).wait_send()
        if dy != 2:
            for z in range(2):
                spread(behind(2, z), dy).wait_send()

    def handed_on(c, _):
        hand_on(c).wait_send()
        return 0

    lax.fori_loop(0, CHIPS, handed_on, 0)


def shards(queries, keys, values, step_sizes, starts, resets, init_in, init_out, gain, out_proj):
    anywhere = pl.BlockSpec(memory_space=pl.ANY)
    vmem = pl.BlockSpec(memory_space=pltpu.VMEM)
    smem = pl.BlockSpec(memory_space=pltpu.SMEM)
    dma = pltpu.SemaphoreType.DMA
    half = jax.ShapeDtypeStruct((VIDEOS, ROWS, OUT), BF16)
    own, part = pl.pallas_call(
        body,
        name="layer",
        out_shape=(half, half),
        in_specs=[smem, smem, vmem, vmem] + [anywhere] * 6,
        out_specs=(anywhere, anywhere),
        scratch_shapes=[
            pltpu.VMEM((VIDEOS, ROWS, 2 * HS), BF16),
            pltpu.VMEM((HS, 2 * HID), BF16),
            pltpu.VMEM((HID, HS), BF16),
            pltpu.VMEM((CHIPS, ROWS, HS), BF16),
            pltpu.VMEM((SEGS, 2, ROWS, HS), BF16),
            pltpu.VMEM((SEGS, 2, HS, ROWS), BF16),
            pltpu.VMEM((CHIPS, ROWS, HS), BF16),
            pltpu.VMEM((SEGS + 1, HS, 2 * HID), BF16),
            pltpu.VMEM((SEGS + 1, HS, HID), BF16),
            pltpu.VMEM((CHIPS, ROWS, HS), BF16),
            pltpu.VMEM((VIDEOS, ROWS, 4 * 2 * HS), BF16),
            pltpu.VMEM((4 * 2 * HS, SLAB), BF16),
            pltpu.VMEM((VIDEOS, ROWS, OUT), BF16),
            pltpu.VMEM((VIDEOS, ROWS, OUT), BF16),
            dma((7,)),
            dma((CHIPS, 2)), dma((CHIPS, 2)),
            dma((CHIPS,)), dma((CHIPS,)),
            dma((CHIPS,)), dma((CHIPS,)),
            dma((CHIPS,)), dma((CHIPS,)),
            dma((4, CHIPS)), dma((4, CHIPS)),
            dma((4,)), dma((4,)),
            dma((4,)), dma((4,)),
            dma((VIDEOS,)), dma((VIDEOS,)), dma((VIDEOS,)),
        ],
        compiler_params=pltpu.CompilerParams(
            collective_id=0, has_side_effects=True, vmem_limit_bytes=60 * 1024 * 1024
        ),
    )(
        starts, resets, gain.reshape(1, 2 * HS), jnp.transpose(step_sizes, (0, 2, 1)),
        queries, keys, values, init_in, init_out, out_proj,
    )
    return (own.astype(F32) + part.astype(F32)).astype(BF16)


def solution(mesh):
    rows = P(None, "frame", "head")
    return jax.shard_map(
        shards,
        mesh=mesh,
        in_specs=(
            rows, rows, rows, rows, P(), P(),
            P("head", None, None), P("head", None, None), P("head"), P("head", None),
        ),
        out_specs=rows,
        check_vma=False,
    )
```

```python
import jax
import jax.numpy as jnp
from jax import lax
from jax.experimental import pallas as pl
from jax.experimental.pallas import tpu as pltpu
from jax.sharding import PartitionSpec as P

MESH = pl.DeviceIdType.MESH
BF16 = jnp.bfloat16
F32 = jnp.float32

VIDEOS = 4
ROWS = 256
SEGS = 16
HS = 256
HID = 512
CHIPS = 8
FRONT = ((1, 1), (3, 0), (3, 1), (1, 0), (2, 0), (0, 1), (2, 1))
WINDOW = 4
SLAB = 1280
OUT = 640
HALF = ROWS // 2


def tile(start, size):
    return pl.ds(pl.multiple_of(start, size), size)


def dot(a, b):
    return jnp.dot(a, b, preferred_element_type=F32)


def dot_t(a, b):
    return lax.dot_general(a, b, (((1,), (1,)), ((), ())), preferred_element_type=F32)


def sigmoid(x):
    return 0.5 * jnp.tanh(0.5 * x) + 0.5


def body(
    starts, resets, gain, steps, queries, keys, values, init_in, init_out, proj,
    own_out, part_out,
    v_buf, init_in_buf, init_out_buf, scaled, ks, kst, q_buf, state_in, state_out,
    normed, a_buf, slab, part_send, own,
    local_sem, ks_send, ks_recv, fwd_send, fwd_recv, q_send, q_recv,
    a_send, a_recv, y_send, y_recv, w_send, w_recv, wf_send, wf_recv, z_send, z_recv, own_sem,
    half_send, half_recv,
):
    frame = lax.axis_index("frame")
    head = lax.axis_index("head")
    chip, core = frame // 2, frame % 2
    y, zl = head // 2, head % 2
    sibling = (chip * 2 + 1 - core, head)
    video, hh = chip // 2, chip % 2

    def peer(c):
        return (c * 2 + core, head)

    def ahead(dx, dz):
        return (video + dx) % 4 * 2 + (hh + dz) % 2

    def behind(dx, dz):
        return (video + 4 - dx) % 4 * 2 + (hh + 2 - dz) % 2

    def y_peer(dy):
        return (frame, ((y + dy) % 4) * 2 + zl)

    z_peer = (frame, y * 2 + 1 - zl)

    def remote(src, dst, send, recv, where):
        return pltpu.make_async_remote_copy(
            src_ref=src, dst_ref=dst, send_sem=send, recv_sem=recv,
            device_id=where, device_id_type=MESH,
        )

    v_copy = pltpu.make_async_copy(values, v_buf, local_sem.at[0])
    ii_copy = pltpu.make_async_copy(init_in.at[hh], init_in_buf, local_sem.at[1])
    io_copy = pltpu.make_async_copy(init_out.at[hh], init_out_buf, local_sem.at[2])
    k_copy = pltpu.make_async_copy(
        keys.at[video, :, tile(hh * HS, HS)], ks.at[frame, 0], local_sem.at[3]
    )
    q_copy = pltpu.make_async_copy(
        queries.at[video, :, tile(hh * HS, HS)], q_buf.at[chip], local_sem.at[4]
    )
    w_copy = pltpu.make_async_copy(
        proj.at[:, tile(y * SLAB, SLAB)], slab.at[tile(y * 2 * HS, 2 * HS)], local_sem.at[5]
    )
    own_copy = pltpu.make_async_copy(
        normed.at[chip], a_buf.at[video, :, tile((y * 2 + hh) * HS, HS)], local_sem.at[6]
    )
    v_copy.start()
    k_copy.start()
    ii_copy.start()
    io_copy.start()
    q_copy.start()

    barrier = pltpu.get_barrier_semaphore()

    def greet(d, _):
        pl.semaphore_signal(barrier, inc=1, device_id=peer((chip + d) % CHIPS), device_id_type=MESH)
        return 0

    lax.fori_loop(1, CHIPS, greet, 0)
    pl.semaphore_signal(barrier, inc=1, device_id=sibling, device_id_type=MESH)
    pl.semaphore_signal(barrier, inc=1, device_id=z_peer, device_id_type=MESH)
    for dy in (1, 2, 3):
        pl.semaphore_signal(barrier, inc=1, device_id=y_peer(dy), device_id_type=MESH)
    pl.semaphore_wait(barrier, CHIPS - 1 + 5)

    def key_to(c):
        return remote(
            keys.at[c // 2, :, tile((c % 2) * HS, HS)], ks.at[frame, 0],
            ks_send.at[c, 0], ks_recv.at[chip, 0], peer(c),
        )

    def scaled_to(c):
        return remote(
            scaled.at[c], ks.at[frame, 1], ks_send.at[c, 1], ks_recv.at[chip, 1], peer(c)
        )

    def query_to(c):
        return remote(
            queries.at[c // 2, :, tile((c % 2) * HS, HS)], q_buf.at[chip],
            q_send.at[c], q_recv.at[chip], peer(c),
        )

    for shift in FRONT[:WINDOW]:
        key_to(ahead(*shift)).start()

    def slab_rows(group, c):
        return slab.at[tile((group * 2 + c) * HS, HS)]

    def slab_to(dy):
        target = (y + dy) % 4
        return remote(
            proj.at[tile(core * HS, HS), tile(target * SLAB, SLAB)], slab_rows(y, core),
            w_send.at[dy], w_recv.at[y], y_peer(dy),
        )

    def slab_from(dy):
        group = (y + dy) % 4
        return remote(
            slab_rows(group, core), slab_rows(group, core),
            w_send.at[dy], w_recv.at[group], y_peer(dy),
        )

    def slab_on(dy):
        group = (y + dy) % 4
        return remote(
            slab_rows(group, core), slab_rows(group, core),
            wf_send.at[dy], wf_recv.at[group], sibling,
        )

    def slab_off(dy):
        group = (y + dy) % 4
        return remote(
            slab_rows(group, 1 - core), slab_rows(group, 1 - core),
            wf_send.at[dy], wf_recv.at[group], sibling,
        )

    v_copy.wait()
    rates = jnp.concatenate([steps[b].astype(F32) for b in range(VIDEOS)], axis=0).T
    for c in range(CHIPS):
        block = v_buf[c // 2, :, (c % 2) * HS : (c % 2 + 1) * HS].astype(F32)
        scaled[c] = (block * rates[:, c : c + 1]).astype(BF16)
    for shift in FRONT[:WINDOW]:
        scaled_to(ahead(*shift)).start()
    w_copy.start()
    for dy in (1, 3, 2):
        slab_to(dy).start()

    ks[frame, 1] = scaled[chip]
    k_copy.wait()

    def hand_on(c):
        slot = c * 2 + core
        return remote(ks.at[slot], ks.at[slot], fwd_send.at[c], fwd_recv.at[c], sibling)

    def handed(c):
        slot = c * 2 + 1 - core
        return remote(ks.at[slot], ks.at[slot], fwd_send.at[c], fwd_recv.at[c], sibling)

    hand_on(chip).start()
    ii_copy.wait()
    io_copy.wait()
    state_in[SEGS] = init_in_buf[...]
    state_out[SEGS] = init_out_buf[...].T
    wide = init_in_buf[...].astype(F32)
    norm_in = jnp.sqrt(jnp.sum(wide * wide, axis=0, keepdims=True))
    wide = state_out[SEGS].astype(F32)
    norm_out = jnp.sqrt(jnp.sum(wide * wide, axis=1, keepdims=True))

    def turn(slot):
        kst[slot, 0] = ks[slot, 0].T
        kst[slot, 1] = ks[slot, 1].T

    turn(frame)

    def key_from(c, which):
        slot = c * 2 + core
        return remote(
            ks.at[slot, which], ks.at[slot, which], ks_send.at[0, which], ks_recv.at[c, which], peer(c)
        )

    def take_handed(c):
        handed(c).wait_recv()
        turn(c * 2 + 1 - core)

    back = chip
    for n, shift in enumerate(FRONT):
        c = behind(*shift)
        key_from(c, 0).wait_recv()
        key_from(c, 1).wait_recv()
        hand_on(c).start()
        if n + WINDOW < len(FRONT):
            done, later = ahead(*shift), ahead(*FRONT[n + WINDOW])
            key_to(done).wait_send()
            scaled_to(done).wait_send()
            key_to(later).start()
            scaled_to(later).start()
        turn(c * 2 + core)
        take_handed(back)
        back = c
    for shift in FRONT:
        query_to(ahead(*shift)).start()
    take_handed(back)

    start = starts[video]

    def segment(s, _):
        block = lax.rem(start + s, SEGS)
        restart = jnp.logical_or(s == 0, resets[video, s] == 1)
        before = jnp.where(restart, SEGS, s - 1)
        key, scl = ks[block, 0], ks[block, 1]
        w_in = state_in[before]
        w_out = state_out[before]
        pre = dot(key, w_in)
        grad = dot(scl, w_out)
        h1, h3 = pre[:, :HID], pre[:, HID:]
        sig = sigmoid(h1)
        act = h1 * sig
        hidden = (act * h3).astype(BF16)
        d1 = (grad * h3 * (sig + act * (1.0 - sig))).astype(BF16)
        d3 = (grad * act).astype(BF16)
        raw_out = w_out.astype(F32) + dot(kst[block, 1], hidden)
        scale = norm_out * lax.rsqrt(jnp.sum(raw_out * raw_out, axis=1, keepdims=True) + 1e-06)
        state_out[s] = (raw_out * scale).astype(BF16)
        turned = kst[block, 0]
        for half, d in ((0, d1), (1, d3)):
            at = slice(half * HID, (half + 1) * HID)
            raw = w_in[:, at].astype(F32) + dot(turned, d)
            scale = norm_in[:, at] * lax.rsqrt(jnp.sum(raw * raw, axis=0, keepdims=True) + 1e-06)
            state_in[s, :, at] = (raw * scale).astype(BF16)
        return 0

    lax.fori_loop(0, SEGS, segment, 0)

    for dy in (1, 3, 2):
        slab_from(dy).wait_recv()
        slab_on(dy).start()

    def query_from(c):
        return remote(q_buf.at[c], q_buf.at[c], q_send.at[c], q_recv.at[c], peer(c))

    def columns_of(group, c):
        return a_buf.at[c // 2, :, tile((group * 2 + c % 2) * HS, HS)]

    def normed_to(c):
        return remote(
            normed.at[c], columns_of(y, chip), a_send.at[c], a_recv.at[chip], peer(c)
        )

    def normed_from(c):
        return remote(
            columns_of(y, c), columns_of(y, c), a_send.at[c], a_recv.at[c], peer(c)
        )

    def spread(c, dy):
        return remote(
            columns_of(y, c), columns_of(y, c), y_send.at[dy, c], y_recv.at[y, c], y_peer(dy)
        )

    def gathered(c, group):
        return remote(
            columns_of(group, c), columns_of(group, c),
            y_send.at[0, c], y_recv.at[group, c], y_peer(1),
        )

    gain_row = jnp.where(hh == 0, gain[:, :HS], gain[:, HS:])

    def query(c):
        done = lax.rem(c * 2 + core + SEGS - start, SEGS)
        pre = dot(q_buf[c], state_in[done])
        h1, h3 = pre[:, :HID], pre[:, HID:]
        hidden = (h1 * sigmoid(h1) * h3).astype(BF16)
        fast = dot_t(hidden, state_out[done])
        fast = fast * lax.rsqrt(jnp.mean(fast * fast, axis=1, keepdims=True) + 1e-05)
        normed[c] = (fast * gain_row).astype(BF16)

    def answer(c):
        query_from(c).wait_recv()
        query(c)
        normed_to(c).start()

    def answer_sides(n, _):
        answer(ahead(1 + n % 2 * 2, n // 2))
        return 0

    def answer_far(n, _):
        answer(ahead(2, n))
        return 0

    def nth(pair):
        return pair + pair // 2 - pair // 3 * 2

    def spread_all(c):
        for dy in (1, 3):
            spread(c, dy).start()

    def relay(c):
        group = (y + 3 + c % 2 * 2) % 4
        return remote(
            columns_of(group, c), columns_of(group, c),
            y_send.at[2, c], y_recv.at[group, c], (frame, ((y + 1 + c % 2 * 2) % 4) * 2 + zl),
        )

    def relay_on(n):
        c = behind(nth(n // 2), n % 2)
        gathered(c, (y + 3 + c % 2 * 2) % 4).wait_recv()
        relay(c).start()

    def pass_on(n):
        c = behind(nth(n // 2), n % 2)
        normed_from(c).wait_recv()

        @pl.when(n > 1)
        def _():
            earlier = behind(nth((n - 2) // 2), n % 2)
            for dy in (1, 3):
                spread(earlier, dy).wait_send()

        spread_all(c)

    def part_to(b):
        return remote(part_send.at[b], part_out.at[b], z_send.at[b], z_recv.at[b], z_peer)

    def own_to(b):
        return pltpu.make_async_copy(own.at[b], own_out.at[b], own_sem.at[b])

    def multiply(b, at):
        rows = a_buf[b, at]
        part_send[b, at] = dot(rows, slab[:, tile((1 - zl) * OUT, OUT)]).astype(BF16)
        return rows

    def multiply_own(b, at, rows):
        own[b, at] = dot(rows, slab[:, tile(zl * OUT, OUT)]).astype(BF16)

    def project(n):
        b = (video + 4 - nth(n)) % 4
        for h in range(2):
            for dy in (2, 1 + 2 * h):
                gathered(b * 2 + h, (y + dy) % 4).wait_recv()
        rows = multiply(b, slice(0, ROWS))
        part_to(b).start()
        multiply_own(b, slice(0, ROWS), rows)
        own_to(b).start()

    last = (video + 2) % 4

    def columns_half(group, h, r):
        return a_buf.at[last, pl.ds(r * HALF, HALF), tile((group * 2 + h) * HS, HS)]

    def spread_half(h, r, dy):
        ref = columns_half(y, h, r)
        return remote(ref, ref, half_send.at[dy, h, r], half_recv.at[y, h, r], y_peer(dy))

    def gathered_half(group, h, r):
        ref = columns_half(group, h, r)
        return remote(ref, ref, half_send.at[0, h, r], half_recv.at[group, h, r], y_peer(1))

    def relay_half(h, r):
        group = (y + 3 + h * 2) % 4
        ref = columns_half(group, h, r)
        return remote(
            ref, ref, half_send.at[2, h, r], half_recv.at[group, h, r], y_peer(1 + h * 2)
        )

    def part_half(r):
        at = pl.ds(r * HALF, HALF)
        where = last if r == 0 else VIDEOS
        return remote(
            part_send.at[last, at], part_out.at[last, at], z_send.at[where], z_recv.at[where], z_peer
        )

    def finish_half(r):
        for h in range(2):
            gathered_half((y + 3 + h * 2) % 4, h, r).wait_recv()
            relay_half(h, r).start()
        for h in range(2):
            for dy in (1 + 2 * h, 2):
                gathered_half((y + dy) % 4, h, r).wait_recv()
        at = slice(r * HALF, (r + 1) * HALF)
        rows = multiply(last, at)
        part_half(r).start()
        return at, rows

    q_copy.wait()
    query(chip)
    own_copy.start()
    own_copy.wait()
    spread_all(chip)
    answer(ahead(0, 1))
    lax.fori_loop(0, 4, answer_sides, 0)
    lax.fori_loop(0, 2, answer_far, 0)
    w_copy.wait()
    for dy in (1, 2, 3):
        slab_off(dy).wait_recv()

    def turns(n, _):
        @pl.when(n < CHIPS - 2)
        def _():
            pass_on(n)

        @pl.when(n < CHIPS - 1)
        def _():
            relay_on(n - 1)

        @pl.when(n == CHIPS - 2)
        def _():
            even, odd = last * 2, last * 2 + 1
            for c in (even, odd):
                normed_from(c).wait_recv()
            for z in range(2):
                for dy in (1, 3):
                    spread(behind(3, z), dy).wait_send()
            for r in range(2):
                for h in range(2):
                    for dy in (1, 3):
                        spread_half(h, r, dy).start()

        @pl.when(jnp.logical_and(n >= 3, n % 2 == 1))
        def _():
            project((n - 3) // 2)

        return 0

    lax.fori_loop(1, CHIPS, turns, 0)
    at, rows = finish_half(0)
    multiply_own(last, at, rows)
    at, rows = finish_half(1)
    multiply_own(last, at, rows)
    own_to(last).start()

    def finish(n, _):
        b = (video + 4 - nth(n)) % 4
        part_to(b).wait_recv()
        own_to(b).wait()
        part_to(b).wait_send()
        return 0

    lax.fori_loop(0, VIDEOS - 1, finish, 0)
    own_to(last).wait()
    for r in range(2):
        part_half(r).wait_recv()
        part_half(r).wait_send()

    for shift in FRONT[len(FRONT) - WINDOW :]:
        key_to(ahead(*shift)).wait_send()
        scaled_to(ahead(*shift)).wait_send()

    def sent(d, _):
        c = (chip + d) % CHIPS
        query_to(c).wait_send()
        normed_to(c).wait_send()
        return 0

    lax.fori_loop(1, CHIPS, sent, 0)

    def relayed(n, _):
        relay(behind(nth(n // 2), n % 2)).wait_send()
        return 0

    lax.fori_loop(0, CHIPS - 2, relayed, 0)
    for r in range(2):
        for h in range(2):
            relay_half(h, r).wait_send()
            for dy in (1, 3):
                spread_half(h, r, dy).wait_send()
    for dy in (1, 2, 3):
        slab_to(dy).wait_send()
        slab_on(dy).wait_send()

    def handed_on(c, _):
        hand_on(c).wait_send()
        return 0

    lax.fori_loop(0, CHIPS, handed_on, 0)


def shards(queries, keys, values, step_sizes, starts, resets, init_in, init_out, gain, out_proj):
    anywhere = pl.BlockSpec(memory_space=pl.ANY)
    vmem = pl.BlockSpec(memory_space=pltpu.VMEM)
    smem = pl.BlockSpec(memory_space=pltpu.SMEM)
    dma = pltpu.SemaphoreType.DMA
    half = jax.ShapeDtypeStruct((VIDEOS, ROWS, OUT), BF16)
    own, part = pl.pallas_call(
        body,
        name="layer",
        out_shape=(half, half),
        in_specs=[smem, smem, vmem, vmem] + [anywhere] * 6,
        out_specs=(anywhere, anywhere),
        scratch_shapes=[
            pltpu.VMEM((VIDEOS, ROWS, 2 * HS), BF16),
            pltpu.VMEM((HS, 2 * HID), BF16),
            pltpu.VMEM((HID, HS), BF16),
            pltpu.VMEM((CHIPS, ROWS, HS), BF16),
            pltpu.VMEM((SEGS, 2, ROWS, HS), BF16),
            pltpu.VMEM((SEGS, 2, HS, ROWS), BF16),
            pltpu.VMEM((CHIPS, ROWS, HS), BF16),
            pltpu.VMEM((SEGS + 1, HS, 2 * HID), BF16),
            pltpu.VMEM((SEGS + 1, HS, HID), BF16),
            pltpu.VMEM((CHIPS, ROWS, HS), BF16),
            pltpu.VMEM((VIDEOS, ROWS, 4 * 2 * HS), BF16),
            pltpu.VMEM((4 * 2 * HS, SLAB), BF16),
            pltpu.VMEM((VIDEOS, ROWS, OUT), BF16),
            pltpu.VMEM((VIDEOS, ROWS, OUT), BF16),
            dma((7,)),
            dma((CHIPS, 2)), dma((CHIPS, 2)),
            dma((CHIPS,)), dma((CHIPS,)),
            dma((CHIPS,)), dma((CHIPS,)),
            dma((CHIPS,)), dma((CHIPS,)),
            dma((4, CHIPS)), dma((4, CHIPS)),
            dma((4,)), dma((4,)),
            dma((4,)), dma((4,)),
            dma((VIDEOS + 1,)), dma((VIDEOS + 1,)), dma((VIDEOS,)),
            dma((4, 2, 2)), dma((4, 2, 2)),
        ],
        compiler_params=pltpu.CompilerParams(
            collective_id=0, has_side_effects=True, vmem_limit_bytes=60 * 1024 * 1024
        ),
    )(
        starts, resets, gain.reshape(1, 2 * HS), jnp.transpose(step_sizes, (0, 2, 1)),
        queries, keys, values, init_in, init_out, out_proj,
    )
    return (own.astype(F32) + part.astype(F32)).astype(BF16)


def solution(mesh):
    rows = P(None, "frame", "head")
    return jax.shard_map(
        shards,
        mesh=mesh,
        in_specs=(
            rows, rows, rows, rows, P(), P(),
            P("head", None, None), P("head", None, None), P("head"), P("head", None),
        ),
        out_specs=rows,
        check_vma=False,
    )
```

```python
import jax
import jax.numpy as jnp
from jax import lax
from jax.experimental import pallas as pl
from jax.experimental.pallas import tpu as pltpu
from jax.sharding import PartitionSpec as P

MESH = pl.DeviceIdType.MESH
BF16 = jnp.bfloat16
F32 = jnp.float32

VIDEOS = 4
ROWS = 256
SEGS = 16
HS = 256
HID = 512
CHIPS = 8
FRONT = ((1, 1), (3, 0), (3, 1), (1, 0), (2, 0), (0, 1), (2, 1))
WINDOW = 4
SLAB = 1280
OUT = 640
HALF = ROWS // 2


def tile(start, size):
    return pl.ds(pl.multiple_of(start, size), size)


def dot(a, b):
    return jnp.dot(a, b, preferred_element_type=F32)


def dot_t(a, b):
    return lax.dot_general(a, b, (((1,), (1,)), ((), ())), preferred_element_type=F32)


def sigmoid(x):
    return 0.5 * jnp.tanh(0.5 * x) + 0.5


def body(
    starts, resets, gain, steps, queries, keys, values, init_in, init_out, proj,
    own_out, part_out,
    v_buf, init_in_buf, init_out_buf, scaled, ks, kst, q_buf, state_in, state_out,
    normed, a_buf, slab, part_send, own,
    local_sem, ks_send, ks_recv, fwd_send, fwd_recv, q_send, q_recv,
    a_send, a_recv, y_send, y_recv, w_send, w_recv, wf_send, wf_recv, z_send, z_recv, own_sem,
    half_send, half_recv,
):
    frame = lax.axis_index("frame")
    head = lax.axis_index("head")
    chip, core = frame // 2, frame % 2
    y, zl = head // 2, head % 2
    sibling = (chip * 2 + 1 - core, head)
    video, hh = chip // 2, chip % 2

    def peer(c):
        return (c * 2 + core, head)

    def ahead(dx, dz):
        return (video + dx) % 4 * 2 + (hh + dz) % 2

    def behind(dx, dz):
        return (video + 4 - dx) % 4 * 2 + (hh + 2 - dz) % 2

    def y_peer(dy):
        return (frame, ((y + dy) % 4) * 2 + zl)

    z_peer = (frame, y * 2 + 1 - zl)

    def remote(src, dst, send, recv, where):
        return pltpu.make_async_remote_copy(
            src_ref=src, dst_ref=dst, send_sem=send, recv_sem=recv,
            device_id=where, device_id_type=MESH,
        )

    v_copy = pltpu.make_async_copy(values, v_buf, local_sem.at[0])
    ii_copy = pltpu.make_async_copy(init_in.at[hh], init_in_buf, local_sem.at[1])
    io_copy = pltpu.make_async_copy(init_out.at[hh], init_out_buf, local_sem.at[2])
    k_copy = pltpu.make_async_copy(
        keys.at[video, :, tile(hh * HS, HS)], ks.at[frame, 0], local_sem.at[3]
    )
    q_copy = pltpu.make_async_copy(
        queries.at[video, :, tile(hh * HS, HS)], q_buf.at[chip], local_sem.at[4]
    )
    w_copy = pltpu.make_async_copy(
        proj.at[:, tile(y * SLAB, SLAB)], slab.at[tile(y * 2 * HS, 2 * HS)], local_sem.at[5]
    )
    own_copy = pltpu.make_async_copy(
        normed.at[chip], a_buf.at[video, :, tile((y * 2 + hh) * HS, HS)], local_sem.at[6]
    )
    v_copy.start()
    k_copy.start()
    ii_copy.start()
    io_copy.start()
    q_copy.start()

    barrier = pltpu.get_barrier_semaphore()

    def greet(d, _):
        pl.semaphore_signal(barrier, inc=1, device_id=peer((chip + d) % CHIPS), device_id_type=MESH)
        return 0

    lax.fori_loop(1, CHIPS, greet, 0)
    pl.semaphore_signal(barrier, inc=1, device_id=sibling, device_id_type=MESH)
    pl.semaphore_signal(barrier, inc=1, device_id=z_peer, device_id_type=MESH)
    for dy in (1, 2, 3):
        pl.semaphore_signal(barrier, inc=1, device_id=y_peer(dy), device_id_type=MESH)
    pl.semaphore_wait(barrier, CHIPS - 1 + 5)

    def key_to(c):
        return remote(
            keys.at[c // 2, :, tile((c % 2) * HS, HS)], ks.at[frame, 0],
            ks_send.at[c, 0], ks_recv.at[chip, 0], peer(c),
        )

    def scaled_to(c):
        return remote(
            scaled.at[c], ks.at[frame, 1], ks_send.at[c, 1], ks_recv.at[chip, 1], peer(c)
        )

    def query_to(c):
        return remote(
            queries.at[c // 2, :, tile((c % 2) * HS, HS)], q_buf.at[chip],
            q_send.at[c], q_recv.at[chip], peer(c),
        )

    for shift in FRONT[:WINDOW]:
        key_to(ahead(*shift)).start()

    def slab_rows(group, c):
        return slab.at[tile((group * 2 + c) * HS, HS)]

    def slab_to(dy):
        target = (y + dy) % 4
        return remote(
            proj.at[tile(core * HS, HS), tile(target * SLAB, SLAB)], slab_rows(y, core),
            w_send.at[dy], w_recv.at[y], y_peer(dy),
        )

    def slab_from(dy):
        group = (y + dy) % 4
        return remote(
            slab_rows(group, core), slab_rows(group, core),
            w_send.at[dy], w_recv.at[group], y_peer(dy),
        )

    def slab_on(dy):
        group = (y + dy) % 4
        return remote(
            slab_rows(group, core), slab_rows(group, core),
            wf_send.at[dy], wf_recv.at[group], sibling,
        )

    def slab_off(dy):
        group = (y + dy) % 4
        return remote(
            slab_rows(group, 1 - core), slab_rows(group, 1 - core),
            wf_send.at[dy], wf_recv.at[group], sibling,
        )

    v_copy.wait()
    rates = jnp.concatenate([steps[b].astype(F32) for b in range(VIDEOS)], axis=0).T
    for c in range(CHIPS):
        block = v_buf[c // 2, :, (c % 2) * HS : (c % 2 + 1) * HS].astype(F32)
        scaled[c] = (block * rates[:, c : c + 1]).astype(BF16)
    for shift in FRONT[:WINDOW]:
        scaled_to(ahead(*shift)).start()
    w_copy.start()
    for dy in (1, 3, 2):
        slab_to(dy).start()

    ks[frame, 1] = scaled[chip]
    k_copy.wait()

    def hand_on(c):
        slot = c * 2 + core
        return remote(ks.at[slot], ks.at[slot], fwd_send.at[c], fwd_recv.at[c], sibling)

    def handed(c):
        slot = c * 2 + 1 - core
        return remote(ks.at[slot], ks.at[slot], fwd_send.at[c], fwd_recv.at[c], sibling)

    hand_on(chip).start()
    ii_copy.wait()
    io_copy.wait()
    state_in[SEGS] = init_in_buf[...]
    state_out[SEGS] = init_out_buf[...].T
    wide = init_in_buf[...].astype(F32)
    norm_in = jnp.sqrt(jnp.sum(wide * wide, axis=0, keepdims=True))
    wide = state_out[SEGS].astype(F32)
    norm_out = jnp.sqrt(jnp.sum(wide * wide, axis=1, keepdims=True))

    def turn(slot):
        kst[slot, 0] = ks[slot, 0].T
        kst[slot, 1] = ks[slot, 1].T

    turn(frame)

    def key_from(c, which):
        slot = c * 2 + core
        return remote(
            ks.at[slot, which], ks.at[slot, which], ks_send.at[0, which], ks_recv.at[c, which], peer(c)
        )

    def take_handed(c):
        handed(c).wait_recv()
        turn(c * 2 + 1 - core)

    back = chip
    for n, shift in enumerate(FRONT):
        c = behind(*shift)
        key_from(c, 0).wait_recv()
        key_from(c, 1).wait_recv()
        hand_on(c).start()
        if n + WINDOW < len(FRONT):
            done, later = ahead(*shift), ahead(*FRONT[n + WINDOW])
            key_to(done).wait_send()
            scaled_to(done).wait_send()
            key_to(later).start()
            scaled_to(later).start()
        turn(c * 2 + core)
        take_handed(back)
        back = c
    for shift in FRONT:
        query_to(ahead(*shift)).start()
    take_handed(back)

    start = starts[video]

    def segment(s, _):
        block = lax.rem(start + s, SEGS)
        restart = jnp.logical_or(s == 0, resets[video, s] == 1)
        before = jnp.where(restart, SEGS, s - 1)
        key, scl = ks[block, 0], ks[block, 1]
        w_in = state_in[before]
        w_out = state_out[before]
        pieces = []
        for lo in range(0, HID, HID // 2):
            hi = lo + HID // 2
            h1 = dot(key, w_in[:, lo:hi])
            h3 = dot(key, w_in[:, HID + lo : HID + hi])
            grad = dot(scl, w_out[:, lo:hi])
            sig = sigmoid(h1)
            act = h1 * sig
            hidden = (act * h3).astype(BF16)
            d1 = (grad * h3 * (sig + act * (1.0 - sig))).astype(BF16)
            d3 = (grad * act).astype(BF16)
            pieces.append((hidden, d1, d3))
        hidden, d1, d3 = [jnp.concatenate(p, axis=1) for p in zip(*pieces)]
        raw_out = w_out.astype(F32) + dot(kst[block, 1], hidden)
        scale = norm_out * lax.rsqrt(jnp.sum(raw_out * raw_out, axis=1, keepdims=True) + 1e-06)
        state_out[s] = (raw_out * scale).astype(BF16)
        turned = kst[block, 0]
        for half, d in ((0, d1), (1, d3)):
            at = slice(half * HID, (half + 1) * HID)
            raw = w_in[:, at].astype(F32) + dot(turned, d)
            scale = norm_in[:, at] * lax.rsqrt(jnp.sum(raw * raw, axis=0, keepdims=True) + 1e-06)
            state_in[s, :, at] = (raw * scale).astype(BF16)
        return 0

    lax.fori_loop(0, SEGS, segment, 0)

    for dy in (1, 3, 2):
        slab_from(dy).wait_recv()
        slab_on(dy).start()

    def query_from(c):
        return remote(q_buf.at[c], q_buf.at[c], q_send.at[c], q_recv.at[c], peer(c))

    def columns_of(group, c):
        return a_buf.at[c // 2, :, tile((group * 2 + c % 2) * HS, HS)]

    def normed_to(c):
        return remote(
            normed.at[c], columns_of(y, chip), a_send.at[c], a_recv.at[chip], peer(c)
        )

    def normed_from(c):
        return remote(
            columns_of(y, c), columns_of(y, c), a_send.at[c], a_recv.at[c], peer(c)
        )

    def spread(c, dy):
        return remote(
            columns_of(y, c), columns_of(y, c), y_send.at[dy, c], y_recv.at[y, c], y_peer(dy)
        )

    def gathered(c, group):
        return remote(
            columns_of(group, c), columns_of(group, c),
            y_send.at[0, c], y_recv.at[group, c], y_peer(1),
        )

    gain_row = jnp.where(hh == 0, gain[:, :HS], gain[:, HS:])

    def query(c):
        done = lax.rem(c * 2 + core + SEGS - start, SEGS)
        pre = dot(q_buf[c], state_in[done])
        h1, h3 = pre[:, :HID], pre[:, HID:]
        hidden = (h1 * sigmoid(h1) * h3).astype(BF16)
        fast = dot_t(hidden, state_out[done])
        fast = fast * lax.rsqrt(jnp.mean(fast * fast, axis=1, keepdims=True) + 1e-05)
        normed[c] = (fast * gain_row).astype(BF16)

    def answer(c):
        query_from(c).wait_recv()
        query(c)
        normed_to(c).start()

    def answer_sides(n, _):
        answer(ahead(1 + n % 2 * 2, n // 2))
        return 0

    def answer_far(n, _):
        answer(ahead(2, n))
        return 0

    def nth(pair):
        return pair + pair // 2 - pair // 3 * 2

    def spread_all(c):
        for dy in (1, 3):
            spread(c, dy).start()

    def relay(c):
        group = (y + 3 + c % 2 * 2) % 4
        return remote(
            columns_of(group, c), columns_of(group, c),
            y_send.at[2, c], y_recv.at[group, c], (frame, ((y + 1 + c % 2 * 2) % 4) * 2 + zl),
        )

    def relay_on(n):
        c = behind(nth(n // 2), n % 2)
        gathered(c, (y + 3 + c % 2 * 2) % 4).wait_recv()
        relay(c).start()

    def pass_on(n):
        c = behind(nth(n // 2), n % 2)
        normed_from(c).wait_recv()

        @pl.when(n > 1)
        def _():
            earlier = behind(nth((n - 2) // 2), n % 2)
            for dy in (1, 3):
                spread(earlier, dy).wait_send()

        spread_all(c)

    def part_to(b):
        return remote(part_send.at[b], part_out.at[b], z_send.at[b], z_recv.at[b], z_peer)

    def own_to(b):
        return pltpu.make_async_copy(own.at[b], own_out.at[b], own_sem.at[b])

    def multiply(b, at):
        rows = a_buf[b, at]
        part_send[b, at] = dot(rows, slab[:, tile((1 - zl) * OUT, OUT)]).astype(BF16)

    def multiply_own(b, at, rows):
        own[b, at] = dot(rows, slab[:, tile(zl * OUT, OUT)]).astype(BF16)

    def project(n):
        b = (video + 4 - nth(n)) % 4
        for h in range(2):
            for dy in (2, 1 + 2 * h):
                gathered(b * 2 + h, (y + dy) % 4).wait_recv()
        multiply(b, slice(0, ROWS))
        part_to(b).start()

    last = (video + 2) % 4

    def columns_half(group, h, r):
        return a_buf.at[last, pl.ds(r * HALF, HALF), tile((group * 2 + h) * HS, HS)]

    def spread_half(h, r, dy):
        ref = columns_half(y, h, r)
        return remote(ref, ref, half_send.at[dy, h, r], half_recv.at[y, h, r], y_peer(dy))

    def gathered_half(group, h, r):
        ref = columns_half(group, h, r)
        return remote(ref, ref, half_send.at[0, h, r], half_recv.at[group, h, r], y_peer(1))

    def relay_half(h, r):
        group = (y + 3 + h * 2) % 4
        ref = columns_half(group, h, r)
        return remote(
            ref, ref, half_send.at[2, h, r], half_recv.at[group, h, r], y_peer(1 + h * 2)
        )

    def part_half(r):
        at = pl.ds(r * HALF, HALF)
        where = last if r == 0 else VIDEOS
        return remote(
            part_send.at[last, at], part_out.at[last, at], z_send.at[where], z_recv.at[where], z_peer
        )

    def finish_half(r):
        for h in range(2):
            gathered_half((y + 3 + h * 2) % 4, h, r).wait_recv()
            relay_half(h, r).start()
        for h in range(2):
            for dy in (1 + 2 * h, 2):
                gathered_half((y + dy) % 4, h, r).wait_recv()
        at = slice(r * HALF, (r + 1) * HALF)
        multiply(last, at)
        part_half(r).start()

    q_copy.wait()
    query(chip)
    own_copy.start()
    own_copy.wait()
    spread_all(chip)
    answer(ahead(0, 1))
    lax.fori_loop(0, 4, answer_sides, 0)
    lax.fori_loop(0, 2, answer_far, 0)
    w_copy.wait()
    for dy in (1, 2, 3):
        slab_off(dy).wait_recv()

    def turns(n, _):
        @pl.when(n < CHIPS - 2)
        def _():
            pass_on(n)

        @pl.when(n < CHIPS - 1)
        def _():
            relay_on(n - 1)

        @pl.when(n == CHIPS - 2)
        def _():
            even, odd = last * 2, last * 2 + 1
            for c in (even, odd):
                normed_from(c).wait_recv()
            for z in range(2):
                for dy in (1, 3):
                    spread(behind(3, z), dy).wait_send()
            for r in range(2):
                for h in range(2):
                    for dy in (1, 3):
                        spread_half(h, r, dy).start()

        @pl.when(jnp.logical_and(n >= 3, n % 2 == 1))
        def _():
            project((n - 3) // 2)

        return 0

    lax.fori_loop(1, CHIPS, turns, 0)
    finish_half(0)
    finish_half(1)

    def multiply_rest(b, _):
        multiply_own(b, slice(0, ROWS), a_buf[b])
        own_to(b).start()
        return 0

    lax.fori_loop(0, VIDEOS, multiply_rest, 0)

    def finish(n, _):
        b = (video + 4 - nth(n)) % 4
        part_to(b).wait_recv()
        own_to(b).wait()
        part_to(b).wait_send()
        return 0

    lax.fori_loop(0, VIDEOS - 1, finish, 0)
    own_to(last).wait()
    for r in range(2):
        part_half(r).wait_recv()
        part_half(r).wait_send()

    for shift in FRONT[len(FRONT) - WINDOW :]:
        key_to(ahead(*shift)).wait_send()
        scaled_to(ahead(*shift)).wait_send()

    def sent(d, _):
        c = (chip + d) % CHIPS
        query_to(c).wait_send()
        normed_to(c).wait_send()
        return 0

    lax.fori_loop(1, CHIPS, sent, 0)

    def relayed(n, _):
        relay(behind(nth(n // 2), n % 2)).wait_send()
        return 0

    lax.fori_loop(0, CHIPS - 2, relayed, 0)
    for r in range(2):
        for h in range(2):
            relay_half(h, r).wait_send()
            for dy in (1, 3):
                spread_half(h, r, dy).wait_send()
    for dy in (1, 2, 3):
        slab_to(dy).wait_send()
        slab_on(dy).wait_send()

    def handed_on(c, _):
        hand_on(c).wait_send()
        return 0

    lax.fori_loop(0, CHIPS, handed_on, 0)


def shards(queries, keys, values, step_sizes, starts, resets, init_in, init_out, gain, out_proj):
    anywhere = pl.BlockSpec(memory_space=pl.ANY)
    vmem = pl.BlockSpec(memory_space=pltpu.VMEM)
    smem = pl.BlockSpec(memory_space=pltpu.SMEM)
    dma = pltpu.SemaphoreType.DMA
    half = jax.ShapeDtypeStruct((VIDEOS, ROWS, OUT), BF16)
    own, part = pl.pallas_call(
        body,
        name="layer",
        out_shape=(half, half),
        in_specs=[smem, smem, vmem, vmem] + [anywhere] * 6,
        out_specs=(anywhere, anywhere),
        scratch_shapes=[
            pltpu.VMEM((VIDEOS, ROWS, 2 * HS), BF16),
            pltpu.VMEM((HS, 2 * HID), BF16),
            pltpu.VMEM((HID, HS), BF16),
            pltpu.VMEM((CHIPS, ROWS, HS), BF16),
            pltpu.VMEM((SEGS, 2, ROWS, HS), BF16),
            pltpu.VMEM((SEGS, 2, HS, ROWS), BF16),
            pltpu.VMEM((CHIPS, ROWS, HS), BF16),
            pltpu.VMEM((SEGS + 1, HS, 2 * HID), BF16),
            pltpu.VMEM((SEGS + 1, HS, HID), BF16),
            pltpu.VMEM((CHIPS, ROWS, HS), BF16),
            pltpu.VMEM((VIDEOS, ROWS, 4 * 2 * HS), BF16),
            pltpu.VMEM((4 * 2 * HS, SLAB), BF16),
            pltpu.VMEM((VIDEOS, ROWS, OUT), BF16),
            pltpu.VMEM((VIDEOS, ROWS, OUT), BF16),
            dma((7,)),
            dma((CHIPS, 2)), dma((CHIPS, 2)),
            dma((CHIPS,)), dma((CHIPS,)),
            dma((CHIPS,)), dma((CHIPS,)),
            dma((CHIPS,)), dma((CHIPS,)),
            dma((4, CHIPS)), dma((4, CHIPS)),
            dma((4,)), dma((4,)),
            dma((4,)), dma((4,)),
            dma((VIDEOS + 1,)), dma((VIDEOS + 1,)), dma((VIDEOS,)),
            dma((4, 2, 2)), dma((4, 2, 2)),
        ],
        compiler_params=pltpu.CompilerParams(
            collective_id=0, has_side_effects=True, vmem_limit_bytes=60 * 1024 * 1024
        ),
    )(
        starts, resets, gain.reshape(1, 2 * HS), jnp.transpose(step_sizes, (0, 2, 1)),
        queries, keys, values, init_in, init_out, out_proj,
    )
    return (own.astype(F32) + part.astype(F32)).astype(BF16)


def solution(mesh):
    rows = P(None, "frame", "head")
    return jax.shard_map(
        shards,
        mesh=mesh,
        in_specs=(
            rows, rows, rows, rows, P(), P(),
            P("head", None, None), P("head", None, None), P("head"), P("head", None),
        ),
        out_specs=rows,
        check_vma=False,
    )
```

```python
import jax
import jax.numpy as jnp
from jax import lax
from jax.experimental import pallas as pl
from jax.experimental.pallas import tpu as pltpu
from jax.sharding import PartitionSpec as P

MESH = pl.DeviceIdType.MESH
BF16 = jnp.bfloat16
F32 = jnp.float32

VIDEOS = 4
ROWS = 256
SEGS = 16
HS = 256
HID = 512
CHIPS = 8
FRONT = ((1, 1), (3, 0), (3, 1), (1, 0), (2, 0), (0, 1), (2, 1))
WINDOW = 4
SLAB = 1280
OUT = 640
HALF = ROWS // 2


def tile(start, size):
    return pl.ds(pl.multiple_of(start, size), size)


def dot(a, b):
    return jnp.dot(a, b, preferred_element_type=F32)


def dot_t(a, b):
    return lax.dot_general(a, b, (((1,), (1,)), ((), ())), preferred_element_type=F32)


def sigmoid(x):
    return 0.5 * jnp.tanh(0.5 * x) + 0.5


def body(
    starts, resets, gain, steps, queries, keys, values, init_in, init_out, proj,
    own_out, part_out,
    v_buf, init_in_buf, init_out_buf, scaled, ks, kst, q_buf, state_in, state_out,
    normed, a_buf, slab, part_send, own,
    local_sem, ks_send, ks_recv, fwd_send, fwd_recv, q_send, q_recv,
    a_send, a_recv, y_send, y_recv, w_send, w_recv, wf_send, wf_recv, z_send, z_recv, own_sem,
    half_send, half_recv,
):
    frame = lax.axis_index("frame")
    head = lax.axis_index("head")
    chip, core = frame // 2, frame % 2
    y, zl = head // 2, head % 2
    sibling = (chip * 2 + 1 - core, head)
    video, hh = chip // 2, chip % 2

    def peer(c):
        return (c * 2 + core, head)

    def ahead(dx, dz):
        return (video + dx) % 4 * 2 + (hh + dz) % 2

    def behind(dx, dz):
        return (video + 4 - dx) % 4 * 2 + (hh + 2 - dz) % 2

    def y_peer(dy):
        return (frame, ((y + dy) % 4) * 2 + zl)

    z_peer = (frame, y * 2 + 1 - zl)

    def remote(src, dst, send, recv, where):
        return pltpu.make_async_remote_copy(
            src_ref=src, dst_ref=dst, send_sem=send, recv_sem=recv,
            device_id=where, device_id_type=MESH,
        )

    v_copy = pltpu.make_async_copy(values, v_buf, local_sem.at[0])
    ii_copy = pltpu.make_async_copy(init_in.at[hh], init_in_buf, local_sem.at[1])
    io_copy = pltpu.make_async_copy(init_out.at[hh], init_out_buf, local_sem.at[2])
    k_copy = pltpu.make_async_copy(
        keys.at[video, :, tile(hh * HS, HS)], ks.at[frame, 0], local_sem.at[3]
    )
    q_copy = pltpu.make_async_copy(
        queries.at[video, :, tile(hh * HS, HS)], q_buf.at[chip], local_sem.at[4]
    )
    w_copy = pltpu.make_async_copy(
        proj.at[:, tile(y * SLAB, SLAB)], slab.at[tile(y * 2 * HS, 2 * HS)], local_sem.at[5]
    )
    own_copy = pltpu.make_async_copy(
        normed.at[chip], a_buf.at[video, :, tile((y * 2 + hh) * HS, HS)], local_sem.at[6]
    )
    v_copy.start()
    k_copy.start()
    ii_copy.start()
    io_copy.start()
    q_copy.start()

    barrier = pltpu.get_barrier_semaphore()

    def greet(d, _):
        pl.semaphore_signal(barrier, inc=1, device_id=peer((chip + d) % CHIPS), device_id_type=MESH)
        return 0

    lax.fori_loop(1, CHIPS, greet, 0)
    pl.semaphore_signal(barrier, inc=1, device_id=sibling, device_id_type=MESH)
    pl.semaphore_signal(barrier, inc=1, device_id=z_peer, device_id_type=MESH)
    for dy in (1, 2, 3):
        pl.semaphore_signal(barrier, inc=1, device_id=y_peer(dy), device_id_type=MESH)
    pl.semaphore_wait(barrier, CHIPS - 1 + 5)

    def key_to(c):
        return remote(
            keys.at[c // 2, :, tile((c % 2) * HS, HS)], ks.at[frame, 0],
            ks_send.at[c, 0], ks_recv.at[chip, 0], peer(c),
        )

    def scaled_to(c):
        return remote(
            scaled.at[c], ks.at[frame, 1], ks_send.at[c, 1], ks_recv.at[chip, 1], peer(c)
        )

    def query_to(c):
        return remote(
            queries.at[c // 2, :, tile((c % 2) * HS, HS)], q_buf.at[chip],
            q_send.at[c], q_recv.at[chip], peer(c),
        )

    for shift in FRONT[:WINDOW]:
        key_to(ahead(*shift)).start()

    def slab_rows(group, c):
        return slab.at[tile((group * 2 + c) * HS, HS)]

    def slab_to(dy):
        target = (y + dy) % 4
        return remote(
            proj.at[tile(core * HS, HS), tile(target * SLAB, SLAB)], slab_rows(y, core),
            w_send.at[dy], w_recv.at[y], y_peer(dy),
        )

    def slab_from(dy):
        group = (y + dy) % 4
        return remote(
            slab_rows(group, core), slab_rows(group, core),
            w_send.at[dy], w_recv.at[group], y_peer(dy),
        )

    def slab_on(dy):
        group = (y + dy) % 4
        return remote(
            slab_rows(group, core), slab_rows(group, core),
            wf_send.at[dy], wf_recv.at[group], sibling,
        )

    def slab_off(dy):
        group = (y + dy) % 4
        return remote(
            slab_rows(group, 1 - core), slab_rows(group, 1 - core),
            wf_send.at[dy], wf_recv.at[group], sibling,
        )

    v_copy.wait()
    rates = jnp.concatenate([steps[b].astype(F32) for b in range(VIDEOS)], axis=0).T
    for c in range(CHIPS):
        block = v_buf[c // 2, :, (c % 2) * HS : (c % 2 + 1) * HS].astype(F32)
        scaled[c] = (block * rates[:, c : c + 1]).astype(BF16)
    for shift in FRONT[:WINDOW]:
        scaled_to(ahead(*shift)).start()
    w_copy.start()
    for dy in (1, 3, 2):
        slab_to(dy).start()

    ks[frame, 1] = scaled[chip]
    k_copy.wait()

    def hand_on(c):
        slot = c * 2 + core
        return remote(ks.at[slot], ks.at[slot], fwd_send.at[c], fwd_recv.at[c], sibling)

    def handed(c):
        slot = c * 2 + 1 - core
        return remote(ks.at[slot], ks.at[slot], fwd_send.at[c], fwd_recv.at[c], sibling)

    hand_on(chip).start()
    ii_copy.wait()
    io_copy.wait()
    state_in[SEGS] = init_in_buf[...]
    state_out[SEGS] = init_out_buf[...].T
    wide = init_in_buf[...].astype(F32)
    norm_in = jnp.sqrt(jnp.sum(wide * wide, axis=0, keepdims=True))
    wide = state_out[SEGS].astype(F32)
    norm_out = jnp.sqrt(jnp.sum(wide * wide, axis=1, keepdims=True))

    def turn(slot):
        kst[slot, 0] = ks[slot, 0].T
        kst[slot, 1] = ks[slot, 1].T

    turn(frame)

    def key_from(c, which):
        slot = c * 2 + core
        return remote(
            ks.at[slot, which], ks.at[slot, which], ks_send.at[0, which], ks_recv.at[c, which], peer(c)
        )

    def take_handed(c):
        handed(c).wait_recv()
        turn(c * 2 + 1 - core)

    back = chip
    for n, shift in enumerate(FRONT):
        c = behind(*shift)
        key_from(c, 0).wait_recv()
        key_from(c, 1).wait_recv()
        hand_on(c).start()
        if n + WINDOW < len(FRONT):
            done, later = ahead(*shift), ahead(*FRONT[n + WINDOW])
            key_to(done).wait_send()
            scaled_to(done).wait_send()
            key_to(later).start()
            scaled_to(later).start()
        turn(c * 2 + core)
        take_handed(back)
        back = c
    for shift in FRONT:
        query_to(ahead(*shift)).start()
    take_handed(back)

    start = starts[video]

    def segment(s, _):
        block = lax.rem(start + s, SEGS)
        restart = jnp.logical_or(s == 0, resets[video, s] == 1)
        before = jnp.where(restart, SEGS, s - 1)
        key, scl = ks[block, 0], ks[block, 1]
        w_in = state_in[before]
        w_out = state_out[before]
        pieces = []
        for lo in range(0, HID, HID // 2):
            hi = lo + HID // 2
            h1 = dot(key, w_in[:, lo:hi])
            h3 = dot(key, w_in[:, HID + lo : HID + hi])
            grad = dot(scl, w_out[:, lo:hi])
            sig = sigmoid(h1)
            act = h1 * sig
            hidden = (act * h3).astype(BF16)
            d1 = (grad * h3 * (sig + act * (1.0 - sig))).astype(BF16)
            d3 = (grad * act).astype(BF16)
            pieces.append((hidden, d1, d3))
        hidden, d1, d3 = [jnp.concatenate(p, axis=1) for p in zip(*pieces)]
        raw_out = w_out.astype(F32) + dot(kst[block, 1], hidden)
        scale = norm_out * lax.rsqrt(jnp.sum(raw_out * raw_out, axis=1, keepdims=True) + 1e-06)
        state_out[s] = (raw_out * scale).astype(BF16)
        turned = kst[block, 0]
        for half, d in ((0, d1), (1, d3)):
            at = slice(half * HID, (half + 1) * HID)
            raw = w_in[:, at].astype(F32) + dot(turned, d)
            scale = norm_in[:, at] * lax.rsqrt(jnp.sum(raw * raw, axis=0, keepdims=True) + 1e-06)
            state_in[s, :, at] = (raw * scale).astype(BF16)
        return 0

    lax.fori_loop(0, SEGS, segment, 0)

    for dy in (1, 3, 2):
        slab_from(dy).wait_recv()
        slab_on(dy).start()

    def query_from(c):
        return remote(q_buf.at[c], q_buf.at[c], q_send.at[c], q_recv.at[c], peer(c))

    def columns_of(group, c):
        return a_buf.at[c // 2, :, tile((group * 2 + c % 2) * HS, HS)]

    def normed_to(c):
        return remote(
            normed.at[c], columns_of(y, chip), a_send.at[c], a_recv.at[chip], peer(c)
        )

    def normed_from(c):
        return remote(
            columns_of(y, c), columns_of(y, c), a_send.at[c], a_recv.at[c], peer(c)
        )

    def spread(c, dy):
        return remote(
            columns_of(y, c), columns_of(y, c), y_send.at[dy, c], y_recv.at[y, c], y_peer(dy)
        )

    def gathered(c, group):
        return remote(
            columns_of(group, c), columns_of(group, c),
            y_send.at[0, c], y_recv.at[group, c], y_peer(1),
        )

    gain_row = jnp.where(hh == 0, gain[:, :HS], gain[:, HS:])

    def query(c):
        done = lax.rem(c * 2 + core + SEGS - start, SEGS)
        pre = dot(q_buf[c], state_in[done])
        h1, h3 = pre[:, :HID], pre[:, HID:]
        hidden = (h1 * sigmoid(h1) * h3).astype(BF16)
        fast = dot_t(hidden, state_out[done])
        fast = fast * lax.rsqrt(jnp.mean(fast * fast, axis=1, keepdims=True) + 1e-05)
        normed[c] = (fast * gain_row).astype(BF16)

    def answer(c):
        query_from(c).wait_recv()
        query(c)
        normed_to(c).start()

    def answer_sides(n, _):
        answer(ahead(1 + n % 2 * 2, n // 2))
        return 0

    def answer_far(n, _):
        answer(ahead(2, n))
        return 0

    def nth(pair):
        return pair + pair // 2 - pair // 3 * 2

    def spread_all(c):
        for dy in (1, 3):
            spread(c, dy).start()

    def relay(c):
        group = (y + 3 + c % 2 * 2) % 4
        return remote(
            columns_of(group, c), columns_of(group, c),
            y_send.at[2, c], y_recv.at[group, c], (frame, ((y + 1 + c % 2 * 2) % 4) * 2 + zl),
        )

    def relay_on(n):
        c = behind(nth(n // 2), n % 2)
        gathered(c, (y + 3 + c % 2 * 2) % 4).wait_recv()
        relay(c).start()

    def pass_on(n):
        c = behind(nth(n // 2), n % 2)
        normed_from(c).wait_recv()

        @pl.when(n > 1)
        def _():
            earlier = behind(nth((n - 2) // 2), n % 2)
            for dy in (1, 3):
                spread(earlier, dy).wait_send()

        spread_all(c)

    def part_to(b):
        return remote(part_send.at[b], part_out.at[b], z_send.at[b], z_recv.at[b], z_peer)

    def own_to(b):
        return pltpu.make_async_copy(own.at[b], own_out.at[b], own_sem.at[b])

    def multiply(b, at):
        rows = a_buf[b, at]
        part_send[b, at] = dot(rows, slab[:, tile((1 - zl) * OUT, OUT)]).astype(BF16)

    def multiply_own(b, at, rows):
        own[b, at] = dot(rows, slab[:, tile(zl * OUT, OUT)]).astype(BF16)

    def project(n):
        b = (video + 4 - nth(n)) % 4
        for h in range(2):
            for dy in (2, 1 + 2 * h):
                gathered(b * 2 + h, (y + dy) % 4).wait_recv()
        multiply(b, slice(0, ROWS))
        part_to(b).start()

    last = (video + 2) % 4

    def columns_half(group, h, r):
        return a_buf.at[last, pl.ds(r * HALF, HALF), tile((group * 2 + h) * HS, HS)]

    def spread_half(h, r, dy):
        ref = columns_half(y, h, r)
        return remote(ref, ref, half_send.at[dy, h, r], half_recv.at[y, h, r], y_peer(dy))

    def gathered_half(group, h, r):
        ref = columns_half(group, h, r)
        return remote(ref, ref, half_send.at[0, h, r], half_recv.at[group, h, r], y_peer(1))

    def relay_half(h, r):
        group = (y + 3 + h * 2) % 4
        ref = columns_half(group, h, r)
        return remote(
            ref, ref, half_send.at[2, h, r], half_recv.at[group, h, r], y_peer(1 + h * 2)
        )

    def part_half(r):
        at = pl.ds(r * HALF, HALF)
        where = last if r == 0 else VIDEOS
        return remote(
            part_send.at[last, at], part_out.at[last, at], z_send.at[where], z_recv.at[where], z_peer
        )

    def finish_half(r):
        for h in range(2):
            gathered_half((y + 3 + h * 2) % 4, h, r).wait_recv()
            relay_half(h, r).start()
        for h in range(2):
            for dy in (1 + 2 * h, 2):
                gathered_half((y + dy) % 4, h, r).wait_recv()
        at = slice(r * HALF, (r + 1) * HALF)
        multiply(last, at)
        part_half(r).start()

    q_copy.wait()
    query(chip)
    own_copy.start()
    own_copy.wait()
    spread_all(chip)
    answer(ahead(0, 1))
    lax.fori_loop(0, 4, answer_sides, 0)
    lax.fori_loop(0, 2, answer_far, 0)
    def turns(n, _):
        @pl.when(n < CHIPS - 2)
        def _():
            pass_on(n)

        @pl.when(n < CHIPS - 1)
        def _():
            relay_on(n - 1)

        @pl.when(n == CHIPS - 2)
        def _():
            even, odd = last * 2, last * 2 + 1
            for c in (even, odd):
                normed_from(c).wait_recv()
            for z in range(2):
                for dy in (1, 3):
                    spread(behind(3, z), dy).wait_send()
            for r in range(2):
                for h in range(2):
                    for dy in (1, 3):
                        spread_half(h, r, dy).start()

        @pl.when(n == 3)
        def _():
            w_copy.wait()
            for dy in (1, 2, 3):
                slab_off(dy).wait_recv()

        @pl.when(jnp.logical_and(n >= 3, n % 2 == 1))
        def _():
            project((n - 3) // 2)

        return 0

    lax.fori_loop(1, CHIPS, turns, 0)
    finish_half(0)
    finish_half(1)

    def multiply_rest(b, _):
        multiply_own(b, slice(0, ROWS), a_buf[b])
        own_to(b).start()
        return 0

    lax.fori_loop(0, VIDEOS, multiply_rest, 0)

    def finish(n, _):
        b = (video + 4 - nth(n)) % 4
        part_to(b).wait_recv()
        own_to(b).wait()
        part_to(b).wait_send()
        return 0

    lax.fori_loop(0, VIDEOS - 1, finish, 0)
    own_to(last).wait()
    for r in range(2):
        part_half(r).wait_recv()
        part_half(r).wait_send()

    for shift in FRONT[len(FRONT) - WINDOW :]:
        key_to(ahead(*shift)).wait_send()
        scaled_to(ahead(*shift)).wait_send()

    def sent(d, _):
        c = (chip + d) % CHIPS
        query_to(c).wait_send()
        normed_to(c).wait_send()
        return 0

    lax.fori_loop(1, CHIPS, sent, 0)

    def relayed(n, _):
        relay(behind(nth(n // 2), n % 2)).wait_send()
        return 0

    lax.fori_loop(0, CHIPS - 2, relayed, 0)
    for r in range(2):
        for h in range(2):
            relay_half(h, r).wait_send()
            for dy in (1, 3):
                spread_half(h, r, dy).wait_send()
    for dy in (1, 2, 3):
        slab_to(dy).wait_send()
        slab_on(dy).wait_send()

    def handed_on(c, _):
        hand_on(c).wait_send()
        return 0

    lax.fori_loop(0, CHIPS, handed_on, 0)


def shards(queries, keys, values, step_sizes, starts, resets, init_in, init_out, gain, out_proj):
    anywhere = pl.BlockSpec(memory_space=pl.ANY)
    vmem = pl.BlockSpec(memory_space=pltpu.VMEM)
    smem = pl.BlockSpec(memory_space=pltpu.SMEM)
    dma = pltpu.SemaphoreType.DMA
    half = jax.ShapeDtypeStruct((VIDEOS, ROWS, OUT), BF16)
    own, part = pl.pallas_call(
        body,
        name="layer",
        out_shape=(half, half),
        in_specs=[smem, smem, vmem, vmem] + [anywhere] * 6,
        out_specs=(anywhere, anywhere),
        scratch_shapes=[
            pltpu.VMEM((VIDEOS, ROWS, 2 * HS), BF16),
            pltpu.VMEM((HS, 2 * HID), BF16),
            pltpu.VMEM((HID, HS), BF16),
            pltpu.VMEM((CHIPS, ROWS, HS), BF16),
            pltpu.VMEM((SEGS, 2, ROWS, HS), BF16),
            pltpu.VMEM((SEGS, 2, HS, ROWS), BF16),
            pltpu.VMEM((CHIPS, ROWS, HS), BF16),
            pltpu.VMEM((SEGS + 1, HS, 2 * HID), BF16),
            pltpu.VMEM((SEGS + 1, HS, HID), BF16),
            pltpu.VMEM((CHIPS, ROWS, HS), BF16),
            pltpu.VMEM((VIDEOS, ROWS, 4 * 2 * HS), BF16),
            pltpu.VMEM((4 * 2 * HS, SLAB), BF16),
            pltpu.VMEM((VIDEOS, ROWS, OUT), BF16),
            pltpu.VMEM((VIDEOS, ROWS, OUT), BF16),
            dma((7,)),
            dma((CHIPS, 2)), dma((CHIPS, 2)),
            dma((CHIPS,)), dma((CHIPS,)),
            dma((CHIPS,)), dma((CHIPS,)),
            dma((CHIPS,)), dma((CHIPS,)),
            dma((4, CHIPS)), dma((4, CHIPS)),
            dma((4,)), dma((4,)),
            dma((4,)), dma((4,)),
            dma((VIDEOS + 1,)), dma((VIDEOS + 1,)), dma((VIDEOS,)),
            dma((4, 2, 2)), dma((4, 2, 2)),
        ],
        compiler_params=pltpu.CompilerParams(
            collective_id=0, has_side_effects=True, vmem_limit_bytes=60 * 1024 * 1024
        ),
    )(
        starts, resets, gain.reshape(1, 2 * HS), jnp.transpose(step_sizes, (0, 2, 1)),
        queries, keys, values, init_in, init_out, out_proj,
    )
    return (own.astype(F32) + part.astype(F32)).astype(BF16)


def solution(mesh):
    rows = P(None, "frame", "head")
    return jax.shard_map(
        shards,
        mesh=mesh,
        in_specs=(
            rows, rows, rows, rows, P(), P(),
            P("head", None, None), P("head", None, None), P("head"), P("head", None),
        ),
        out_specs=rows,
        check_vma=False,
    )
```
